128 devices in a mesh: row: 16 (over z, y), col: 8 (over x, core).
Axes of the slice: x: 4, y: 4, z: 4, core: 2. Of those that a mesh axis runs over, the one named last changes fastest.
Arguments:
- sea_fields_now: bfloat16 [480, 1440, 256], P('row', 'col'), may hold values from -6 to 6
- water_site_flags: int32 [480, 1440], P('row', 'col'), may hold values from 0 to 1, as said below
- separable_stencils: bfloat16 [2, 7, 7, 256], replicated, may hold values from -0.875 to 0.875
- sea_scaling_factors: float32 [2, 256], replicated, may hold values from 0.1 to 1.9
- sea_first_matrices: bfloat16 [2, 256, 1024], replicated, may hold values from -0.375 to 0.375
- sea_second_matrices: bfloat16 [2, 1024, 256], replicated, may hold values from -0.1875 to 0.1875
- exchange_to_sea_matrix: float32 [8, 256], replicated, may hold values from -2 to 2
- heat_emitter: bfloat16 [256], replicated, may hold values from -0.375 to 0.375
- air_fields_now: bfloat16 [360, 192, 384], P('col', 'row'), may hold values from -6 to 6
- air_scaling_factors: float32 [2, 384], replicated, may hold values from 0.1 to 1.9
- harmonic_combine_matrix: bfloat16 [96, 384, 384], P('row'), may hold values from -0.3125 to 0.3125
- air_first_matrix: bfloat16 [384, 768], replicated, may hold values from -0.3125 to 0.3125
- air_second_matrix: bfloat16 [768, 384], replicated, may hold values from -0.21875 to 0.21875
- exchange_emitter: bfloat16 [384, 8], replicated, may hold values from -0.3125 to 0.3125
- heat_to_air_matrix: float32 [384], replicated, may hold values from -3 to 3
- regrid_area_factors: bfloat16 [16, 8, 3, 180, 5400], P('row', 'col'), may hold values from -0.25 to 0.25
- link_regrid_group: int32 [16, 8, 3], P(None, 'col'), may hold values from 0 to 47, as said below
- patch_active_links: int32 [16, 8], P(None, 'col'), may hold values from 1 to 3, as said below
Outputs:
- ocean_next: bfloat16 [480, 1440, 256], P('row', 'col')
- air_fields_next: bfloat16 [360, 192, 384], P('col', 'row')
The draws below stay inside these ranges and needn't reach their ends.
Inputs may be any that keep to these rules, and one draw needn't show every extreme that they name: `water_site_flags`: 1 marks an ocean cell, 0 land. `link_regrid_group`: A value q names block q mod 3 of latitude band q // 3 in the tile's own column; the 3 slots of one tile name 3 different bands. Slots p < patch_active_links of a tile are live; some tile has all 3 live in every draw.
All inputs are finite; a program needn't handle non-finite values.
Results may differ from the reference program's by a relative error of at most 0.023.
Values may be sent and summed in bfloat16 or wider, within the bound.
No kernel may reach another device: no remote copies, remote signals or barrier semaphores. Data moves between devices by JAX's collectives and lax.ppermute only.
A program may use at most 192 MiB of HBM per device.

```python
import math
import jax
import jax.numpy as jnp
from jax import lax

SEA_FEATURE_DIM = 256
OHID = 1024
AIR_FEATURE_DIM = 384
AHID = 768
NF = 8
MERIDIAN_TOTAL = 360
MMAX = 96
LMODES = 96
LAYERS = 2
REGRID_GROUPS = 3
PATCH_LINK_ROOM = 3
STRIP_PARALLELS = 12
PATCH_ROWS = 30
PATCH_COLUMNS = 180
NY = 480
NX = 1440
PARALLEL_TOTAL = 192
TILE_ROWS = 16
TILE_COLS = 8
TCELLS = 5400
AIR_SITE_TOTAL = 180
N_ROW = 16
N_COL = 8


def draw_water_site_flags(key, part):
    key = jax.random.fold_in(key, 5)
    rect_total = 24
    keys = jax.random.split(key, 4)
    top_row = jax.random.randint(keys[0], (rect_total,), 0, NY)
    left_col = jax.random.randint(keys[1], (rect_total,), 0, NX)
    rect_rows = jax.random.randint(keys[2], (rect_total,), 1, max(2, NY // 3))
    rect_cols = jax.random.randint(keys[3], (rect_total,), 1, max(2, NX // 3))
    row_index = jnp.arange(NY, dtype=jnp.int32)[:, None, None]
    col_index = jnp.arange(NX, dtype=jnp.int32)[None, :, None]
    inside = (row_index >= top_row) & (row_index < top_row + rect_rows) & (col_index >= left_col) & (col_index < left_col + rect_cols)
    return (1 - jnp.any(inside, axis=-1).astype(jnp.int32)).astype(jnp.int32)


def draw_link_regrid_group(key, part):
    key = jax.random.fold_in(key, 7)
    first_key, second_key = jax.random.split(key)
    scores = jax.random.randint(first_key, (TILE_ROWS, TILE_COLS, N_ROW), 0, 1 << 20) * N_ROW + jnp.arange(N_ROW, dtype=jnp.int32)
    band_order = jnp.argsort(scores, axis=-1, stable=True)[..., :PATCH_LINK_ROOM].astype(jnp.int32)
    block_pick = jax.random.randint(second_key, (TILE_ROWS, TILE_COLS, PATCH_LINK_ROOM), 0, REGRID_GROUPS)
    return (band_order * REGRID_GROUPS + block_pick).astype(jnp.int32)


def draw_patch_active_links(key, part):
    key = jax.random.fold_in(key, 9)
    first_key, second_key = jax.random.split(key)
    counts = jax.random.randint(first_key, (TILE_ROWS, TILE_COLS), 1, PATCH_LINK_ROOM + 1)
    target = jax.random.randint(second_key, (), 0, TILE_ROWS * TILE_COLS)
    flat_index = jnp.arange(TILE_ROWS * TILE_COLS, dtype=jnp.int32).reshape(TILE_ROWS, TILE_COLS)
    return jnp.where(flat_index == target, PATCH_LINK_ROOM, counts).astype(jnp.int32)


def steps_of(key, dims, pieces, least, largest):
    def one(position, parts):
        heights = jax.random.uniform(jax.random.fold_in(jax.random.fold_in(key, 6), position), (parts,), jnp.float32, least / len(pieces), largest / len(pieces))
        return jnp.repeat(jnp.exp(heights), dims[position] // parts).reshape((-1,) + (1,) * (len(dims) - position - 1))

    gain = one(*pieces[0])
    for cut in pieces[1:]:
        gain = gain * one(*cut)
    return gain


def normal_values(key, extent, scale, bound, pieces=(), held_as=jnp.bfloat16):
    values = scale * jax.random.normal(key, extent, jnp.float32)
    if pieces:
        values = values * steps_of(key, extent, pieces, -0.22, 0.18)
    return jnp.clip(values, -bound, bound).astype(held_as)


def setup_inputs(seed: int = 0) -> dict:
    seeds = jax.random.split(jax.random.key(seed), 19)
    sea_fields_now = normal_values(seeds[0], (NY, NX, SEA_FEATURE_DIM), 1.0, 6.0, ((0, 16), (1, 8)))
    water_site_flags = draw_water_site_flags(jax.random.fold_in(seeds[18], 71), 0)
    separable_stencils = normal_values(seeds[2], (LAYERS, 7, 7, SEA_FEATURE_DIM), 49 ** -0.5, 0.875)
    sea_scaling_factors = jnp.clip(1.0 + 0.18 * jax.random.normal(seeds[3], (LAYERS, SEA_FEATURE_DIM), jnp.float32), 0.1, 1.9)
    sea_first_matrices = normal_values(seeds[4], (LAYERS, SEA_FEATURE_DIM, OHID), SEA_FEATURE_DIM ** -0.5, 0.375)
    sea_second_matrices = normal_values(seeds[5], (LAYERS, OHID, SEA_FEATURE_DIM), OHID ** -0.5, 0.1875)
    exchange_to_sea_matrix = normal_values(seeds[6], (NF, SEA_FEATURE_DIM), NF ** -0.5, 2.0, (), jnp.float32)
    heat_emitter = normal_values(seeds[7], (SEA_FEATURE_DIM,), SEA_FEATURE_DIM ** -0.5, 0.375)
    air_fields_now = normal_values(seeds[8], (MERIDIAN_TOTAL, PARALLEL_TOTAL, AIR_FEATURE_DIM), 1.0, 6.0, ((0, 8), (1, 16)))
    air_scaling_factors = jnp.clip(1.0 + 0.18 * jax.random.normal(seeds[9], (2, AIR_FEATURE_DIM), jnp.float32), 0.1, 1.9)
    harmonic_combine_matrix = normal_values(seeds[10], (LMODES, AIR_FEATURE_DIM, AIR_FEATURE_DIM), AIR_FEATURE_DIM ** -0.5, 0.3125, ((0, 16),))
    air_first_matrix = normal_values(seeds[11], (AIR_FEATURE_DIM, AHID), AIR_FEATURE_DIM ** -0.5, 0.3125)
    air_second_matrix = normal_values(seeds[12], (AHID, AIR_FEATURE_DIM), AHID ** -0.5, 0.21875)
    exchange_emitter = normal_values(seeds[13], (AIR_FEATURE_DIM, NF), AIR_FEATURE_DIM ** -0.5, 0.3125)
    heat_to_air_matrix = normal_values(seeds[14], (AIR_FEATURE_DIM,), 0.5, 3.0, (), jnp.float32)
    regrid_area_factors = normal_values(seeds[15], (TILE_ROWS, TILE_COLS, PATCH_LINK_ROOM, AIR_SITE_TOTAL, TCELLS), (PATCH_LINK_ROOM * AIR_SITE_TOTAL) ** -0.5, 0.25, ((0, 16), (1, 8)))
    link_regrid_group = draw_link_regrid_group(jax.random.fold_in(seeds[18], 71), 0)
    patch_active_links = draw_patch_active_links(jax.random.fold_in(seeds[18], 71), 0)
    return dict(sea_fields_now=sea_fields_now, water_site_flags=water_site_flags, separable_stencils=separable_stencils, sea_scaling_factors=sea_scaling_factors, sea_first_matrices=sea_first_matrices, sea_second_matrices=sea_second_matrices, exchange_to_sea_matrix=exchange_to_sea_matrix, heat_emitter=heat_emitter, air_fields_now=air_fields_now, air_scaling_factors=air_scaling_factors, harmonic_combine_matrix=harmonic_combine_matrix, air_first_matrix=air_first_matrix, air_second_matrix=air_second_matrix, exchange_emitter=exchange_emitter, heat_to_air_matrix=heat_to_air_matrix, regrid_area_factors=regrid_area_factors, link_regrid_group=link_regrid_group, patch_active_links=patch_active_links)


EPSILON = 1e-06
HIGHEST_MODE = lax.Precision.HIGHEST

def rescale_features(values, gain_row):
    centred = values - lax.optimization_barrier(jnp.mean(values, axis=-1, keepdims=True))
    spread_sq = lax.optimization_barrier(jnp.mean(centred * centred, axis=-1, keepdims=True))
    return centred * lax.rsqrt(spread_sq + EPSILON) * gain_row

def rounded(values):
    return lax.optimization_barrier(values.astype(jnp.bfloat16)).astype(jnp.float32)

def zonal_table(count_lon, mode_count):
    lon_index = jnp.arange(count_lon, dtype=jnp.int32)[:, None]
    wave_index = jnp.arange(2 * mode_count, dtype=jnp.int32)[None, :]
    phase_step = lon_index * (wave_index % mode_count) % count_lon
    angles = phase_step.astype(jnp.float32) * (2.0 * math.pi / count_lon)
    basis_table = jnp.where(wave_index < mode_count, jnp.cos(angles), jnp.sin(angles))
    return (basis_table * math.sqrt(2.0 / count_lon)).astype(jnp.bfloat16)

def merid_table(count_lat, mode_count):
    lat_index = jnp.arange(count_lat, dtype=jnp.int32)[:, None]
    mode_index = jnp.arange(mode_count, dtype=jnp.int32)[None, :]
    phase_step = (2 * lat_index + 1) * mode_index % (4 * count_lat)
    angles = phase_step.astype(jnp.float32) * (math.pi / (2.0 * count_lat))
    return (jnp.cos(angles) * math.sqrt(2.0 / count_lat)).astype(jnp.bfloat16)

def interface_exchange(air_fields_now, exchange_emitter, sea_fields_now, heat_emitter, water_site_flags, regrid_area_factors, link_regrid_group, patch_active_links):
    meridian_group = MERIDIAN_TOTAL // N_COL // REGRID_GROUPS
    block_total = N_ROW * REGRID_GROUPS
    flux_cells = jnp.dot(air_fields_now.reshape(-1, AIR_FEATURE_DIM), exchange_emitter, preferred_element_type=jnp.float32).astype(jnp.bfloat16)
    flux_cells = flux_cells.reshape(N_COL, REGRID_GROUPS, meridian_group, N_ROW, STRIP_PARALLELS, NF)
    flux_blocks = flux_cells.transpose(0, 3, 1, 5, 2, 4).reshape(N_COL, block_total, NF, AIR_SITE_TOTAL)
    heat_site_values = jnp.dot(sea_fields_now.reshape(-1, SEA_FEATURE_DIM), heat_emitter, preferred_element_type=jnp.float32)
    heat_site_values = (heat_site_values * water_site_flags.reshape(-1).astype(jnp.float32)).astype(jnp.bfloat16)
    heat_patchwise = heat_site_values.reshape(N_ROW, PATCH_ROWS, N_COL, PATCH_COLUMNS).transpose(0, 2, 1, 3).reshape(N_ROW * N_COL, PATCH_ROWS * PATCH_COLUMNS)
    patchwise_factors = regrid_area_factors.reshape(N_ROW * N_COL, PATCH_LINK_ROOM, AIR_SITE_TOTAL, PATCH_ROWS * PATCH_COLUMNS)
    patchwise_links = link_regrid_group.reshape(N_ROW * N_COL, PATCH_LINK_ROOM)
    patchwise_link_totals = patch_active_links.reshape(N_ROW * N_COL)
    patch_vertical_number = jnp.arange(N_ROW * N_COL, dtype=jnp.int32) % N_COL

    def one_patch_work(strip_shares):
        network_parameters, patch_heat_values, own_links, own_link_total, vertical_slot_place = strip_shares
        link_active_flag = jnp.arange(PATCH_LINK_ROOM, dtype=jnp.int32) < own_link_total
        select = (link_active_flag[:, None] & (own_links[:, None] == jnp.arange(block_total, dtype=jnp.int32)[None, :])).astype(jnp.float32)
        blocks_here = lax.dynamic_index_in_dim(flux_blocks, vertical_slot_place, 0, keepdims=False).astype(jnp.float32)
        chosen = jnp.einsum('pq,qfa->pfa', select, blocks_here)
        real_valued_factors = network_parameters.astype(jnp.float32)
        patch_exchange_values = jnp.einsum('pfa,pao->fo', chosen, real_valued_factors)
        link_heat_values = jnp.einsum('hnc,c->hn', real_valued_factors, patch_heat_values.astype(jnp.float32)) * link_active_flag[:, None].astype(jnp.float32)
        return (patch_exchange_values, link_heat_values.astype(jnp.bfloat16))
    patch_exchange_values, link_heat_values = lax.map(one_patch_work, (patchwise_factors, heat_patchwise, patchwise_links, patchwise_link_totals, patch_vertical_number))
    sea_exchange_values = patch_exchange_values.reshape(N_ROW, N_COL, NF, PATCH_ROWS, PATCH_COLUMNS)
    alive_all = jnp.arange(PATCH_LINK_ROOM, dtype=jnp.int32)[None, None, :] < patch_active_links[:, :, None]
    received_store = (alive_all[..., None] & (link_regrid_group[..., None] == jnp.arange(block_total, dtype=jnp.int32))).astype(jnp.float32)
    heat_group_values = jnp.einsum('lmws,lmwq->msq', received_store, link_heat_values.reshape(N_ROW, N_COL, PATCH_LINK_ROOM, AIR_SITE_TOTAL).astype(jnp.float32))
    heat_lattice = heat_group_values.reshape(N_COL, N_ROW, REGRID_GROUPS, meridian_group, STRIP_PARALLELS).transpose(0, 2, 3, 1, 4).reshape(MERIDIAN_TOTAL, PARALLEL_TOTAL)
    return (sea_exchange_values, heat_lattice)

def air_forward_step(air_fields_now, air_scaling_factors, harmonic_combine_matrix, air_first_matrix, air_second_matrix, heat_lattice, heat_to_air_matrix):
    strip_meridian_number = MERIDIAN_TOTAL // N_COL
    wave_total = 2 * MMAX
    state_f = air_fields_now.astype(jnp.float32)
    normed = rescale_features(state_f, air_scaling_factors[0]).astype(jnp.bfloat16)
    zonal_basis = zonal_table(MERIDIAN_TOTAL, MMAX)
    merid_basis = merid_table(PARALLEL_TOTAL, LMODES)

    def lon_piece(running, strip_shares):
        basis_piece, field_piece = strip_shares
        return (running + rounded(jnp.einsum('ok,otc->ktc', basis_piece, field_piece)), None)
    zonal_parts = zonal_basis.reshape(N_COL, strip_meridian_number, wave_total).astype(jnp.float32)
    normed_parts = normed.reshape(N_COL, strip_meridian_number, PARALLEL_TOTAL, AIR_FEATURE_DIM).astype(jnp.float32)
    start_zero = jnp.zeros((wave_total, PARALLEL_TOTAL, AIR_FEATURE_DIM), jnp.float32)
    zonal_coeffs = lax.scan(lon_piece, start_zero, (zonal_parts, normed_parts))[0].astype(jnp.bfloat16)

    def lat_piece(running, strip_shares):
        basis_piece, field_piece = strip_shares
        return (running + rounded(jnp.einsum('tl,ktc->lkc', basis_piece, field_piece)), None)
    merid_parts = merid_basis.reshape(N_ROW, STRIP_PARALLELS, LMODES).astype(jnp.float32)
    coeff_parts = zonal_coeffs.reshape(wave_total, N_ROW, STRIP_PARALLELS, AIR_FEATURE_DIM).transpose(1, 0, 2, 3).astype(jnp.float32)
    start_modes = jnp.zeros((LMODES, wave_total, AIR_FEATURE_DIM), jnp.float32)
    spectra = lax.scan(lat_piece, start_modes, (merid_parts, coeff_parts))[0].astype(jnp.bfloat16)
    filtered = jnp.einsum('lkc,lcd->lkd', spectra.astype(jnp.float32), harmonic_combine_matrix.astype(jnp.float32)).astype(jnp.bfloat16)
    band_coeffs = jnp.einsum('tl,lkc->tkc', merid_basis.astype(jnp.float32), filtered.astype(jnp.float32)).astype(jnp.bfloat16)
    spectral_out = jnp.einsum('nk,tkc->ntc', zonal_basis.astype(jnp.float32), band_coeffs.astype(jnp.float32))
    air_fields_hidden = state_f + spectral_out
    air_fields_entry = rescale_features(air_fields_hidden, air_scaling_factors[1]) + heat_lattice[..., None] * heat_to_air_matrix
    air_fields_entry = air_fields_entry.astype(jnp.bfloat16).reshape(-1, AIR_FEATURE_DIM)
    atmos_hidden = jax.nn.gelu(jnp.dot(air_fields_entry, air_first_matrix, preferred_element_type=jnp.float32), approximate=True).astype(jnp.bfloat16)
    result = air_fields_hidden.reshape(-1, AIR_FEATURE_DIM) + jnp.dot(atmos_hidden, air_second_matrix, preferred_element_type=jnp.float32)
    return result.reshape(MERIDIAN_TOTAL, PARALLEL_TOTAL, AIR_FEATURE_DIM).astype(jnp.bfloat16)

def ocean_layers(sea_fields_now, water_site_flags, separable_stencils, sea_scaling_factors, sea_first_matrices, sea_second_matrices, exchange_to_sea_matrix, sea_exchange_values):
    current = sea_fields_now
    for layer_index in range(LAYERS):
        padded = jnp.pad(current, ((3, 3), (0, 0), (0, 0)))
        padded = jnp.concatenate([padded[:, NX - 3:], padded, padded[:, :3]], axis=1)

        def one_band(band_index, padded=padded, current=current, layer_index=layer_index):
            rows_in = lax.dynamic_slice_in_dim(padded, band_index * PATCH_ROWS, PATCH_ROWS + 6, 0)
            conv_sum = jnp.zeros((PATCH_ROWS, NX, SEA_FEATURE_DIM), jnp.float32)
            for shift_row in range(7):
                for shift_col in range(7):
                    conv_sum = conv_sum + rows_in[shift_row:shift_row + PATCH_ROWS, shift_col:shift_col + NX].astype(jnp.float32) * separable_stencils[layer_index, shift_row, shift_col].astype(jnp.float32)
            normed = rescale_features(conv_sum, sea_scaling_factors[layer_index])
            if layer_index == LAYERS - 1:
                flux_band = lax.dynamic_index_in_dim(sea_exchange_values, band_index, 0, keepdims=False)
                forcing = jnp.einsum('cfyx,fd->ycxd', flux_band, exchange_to_sea_matrix, precision=HIGHEST_MODE).reshape(PATCH_ROWS, NX, SEA_FEATURE_DIM)
                normed = normed + forcing
            normed = normed.astype(jnp.bfloat16).reshape(-1, SEA_FEATURE_DIM)
            hidden = jax.nn.gelu(jnp.dot(normed, sea_first_matrices[layer_index], preferred_element_type=jnp.float32), approximate=True).astype(jnp.bfloat16)
            residual = lax.dynamic_slice_in_dim(current, band_index * PATCH_ROWS, PATCH_ROWS, 0).reshape(-1, SEA_FEATURE_DIM).astype(jnp.float32)
            mask_band = lax.dynamic_slice_in_dim(water_site_flags, band_index * PATCH_ROWS, PATCH_ROWS, 0).reshape(-1).astype(jnp.float32)
            result = (residual + jnp.dot(hidden, sea_second_matrices[layer_index], preferred_element_type=jnp.float32)) * mask_band[:, None]
            return result.reshape(PATCH_ROWS, NX, SEA_FEATURE_DIM).astype(jnp.bfloat16)
        current = lax.map(one_band, jnp.arange(N_ROW, dtype=jnp.int32)).reshape(NY, NX, SEA_FEATURE_DIM)
    return current

def reference(sea_fields_now, water_site_flags, separable_stencils, sea_scaling_factors, sea_first_matrices, sea_second_matrices, exchange_to_sea_matrix, heat_emitter, air_fields_now, air_scaling_factors, harmonic_combine_matrix, air_first_matrix, air_second_matrix, exchange_emitter, heat_to_air_matrix, regrid_area_factors, link_regrid_group, patch_active_links):
    sea_exchange_values, heat_lattice = interface_exchange(air_fields_now, exchange_emitter, sea_fields_now, heat_emitter, water_site_flags, regrid_area_factors, link_regrid_group, patch_active_links)
    air_fields_next = air_forward_step(air_fields_now, air_scaling_factors, harmonic_combine_matrix, air_first_matrix, air_second_matrix, heat_lattice, heat_to_air_matrix)
    ocean_next = ocean_layers(sea_fields_now, water_site_flags, separable_stencils, sea_scaling_factors, sea_first_matrices, sea_second_matrices, exchange_to_sea_matrix, sea_exchange_values)
    return (ocean_next, air_fields_next)
```

```python
import functools
import math

import jax
import jax.numpy as jnp
import numpy as np
from jax import lax
from jax.experimental import pallas as pl
from jax.experimental.pallas import tpu as pltpu
from jax.sharding import PartitionSpec as P

NF = 8
MERIDIAN_TOTAL = 360
MMAX = 96
LMODES = 96
LAYERS = 2
REGRID_GROUPS = 3
PATCH_LINK_ROOM = 3


EPSILON = 1e-06
HIGHEST_MODE = lax.Precision.HIGHEST


def rescale_features(values, gain_row):
    centred = values - jnp.mean(values, axis=-1, keepdims=True)
    spread_sq = jnp.mean(centred * centred, axis=-1, keepdims=True)
    return centred * lax.rsqrt(spread_sq + EPSILON) * gain_row


def zonal_table(count_lon, mode_count):
    lon_index = jnp.arange(count_lon, dtype=jnp.int32)[:, None]
    wave_index = jnp.arange(2 * mode_count, dtype=jnp.int32)[None, :]
    phase_step = lon_index * (wave_index % mode_count) % count_lon
    angles = phase_step.astype(jnp.float32) * (2.0 * math.pi / count_lon)
    basis_table = jnp.where(wave_index < mode_count, jnp.cos(angles), jnp.sin(angles))
    return (basis_table * math.sqrt(2.0 / count_lon)).astype(jnp.bfloat16)


def merid_table(count_lat, mode_count):
    lat_index = jnp.arange(count_lat, dtype=jnp.int32)[:, None]
    mode_index = jnp.arange(mode_count, dtype=jnp.int32)[None, :]
    phase_step = (2 * lat_index + 1) * mode_index % (4 * count_lat)
    angles = phase_step.astype(jnp.float32) * (math.pi / (2.0 * count_lat))
    return (jnp.cos(angles) * math.sqrt(2.0 / count_lat)).astype(jnp.bfloat16)


BF16 = jnp.bfloat16
F32 = jnp.float32
GELU_SLOPE = math.sqrt(2.0 / math.pi)
GELU_SCALE = (GELU_SLOPE * 0.044715) ** (1.0 / 3.0)
GELU_LINEAR = GELU_SLOPE / GELU_SCALE
VMEM_BYTES = 60 * 1024 * 1024
ROWS = 30
COLS = 180
CHANNELS = 256
CHUNK = 10
PREP = 6


def scaled_gelu(scaled):
    inner = (scaled * scaled + GELU_LINEAR) * scaled
    return scaled + scaled * jnp.tanh(inner)


def ocean_tables():
    gather = np.zeros((480, 208), np.float32)
    for shift in range(10):
        for block in range(48):
            place = 4 * block + shift - 3
            if 0 <= place < COLS:
                gather[shift * 48 + block, place] = 1
            elif -3 <= place < 0:
                gather[shift * 48 + block, 192 + place + 3] = 1
            elif COLS <= place < COLS + 3:
                gather[shift * 48 + block, 195 + place - COLS] = 1
    spread = np.zeros((COLS, 192), np.float32)
    for place in range(COLS):
        spread[place, (place % 4) * 48 + place // 4] = 1
    diagonal = np.tile(np.eye(64, dtype=np.float32), (1, 4))
    return gather, spread, diagonal


def expand_taps(taps):
    empty = jnp.zeros((7, CHANNELS), taps.dtype)
    offsets = []
    for offset in range(10):
        offsets.append(
            jnp.stack([taps[:, offset - out] if 0 <= offset - out < 7 else empty for out in range(4)], 1)
        )
    table = jnp.stack(offsets, 1)
    return table.reshape(70, 4, 4, 64).transpose(2, 0, 1, 3).reshape(4, 70, 256)


def ocean_kernel(*refs, forced):
    x, top, bot, halo, gather, taps, diagonal, gain, up, down, mask, spread = refs[:12]
    if forced:
        flux, mixing, out, line, blocks, toeplitz, conv_a, conv_b, normed = refs[12:]
    else:
        out, line, blocks, toeplitz, conv_a, conv_b, normed = refs[12:]
    chunks = ROWS // CHUNK
    lower = lax.broadcasted_iota(jnp.int32, (48, 128), 1) < 64

    def split_row(source, source_row, row, slot):
        line[slot, 0:180] = source[source_row]
        line[slot, 192:208] = halo[row]
        moved = jnp.dot(gather[...], line[slot], preferred_element_type=F32)
        for k in range(5):
            even = moved[96 * k : 96 * k + 48]
            odd = moved[96 * k + 48 : 96 * k + 96]
            for h in range(2):
                e = even[:, 128 * h : 128 * h + 128]
                o = odd[:, 128 * h : 128 * h + 128]
                blocks[2 * h, k, row] = jnp.where(lower, e, pltpu.roll(o, 64, 1)).astype(BF16)
                blocks[2 * h + 1, k, row] = jnp.where(lower, pltpu.roll(e, 64, 1), o).astype(BF16)

    for slot in range(PREP):
        line[slot, 176:192] = jnp.zeros((16, CHANNELS), BF16)
    for row in range(3):
        split_row(top, row, row, row)
        split_row(bot, row, 33 + row, row + 3)

    def split_rows(step, carry):
        for q in range(PREP):
            split_row(x, PREP * step + q, PREP * step + 3 + q, q)
        return carry

    lax.fori_loop(0, ROWS // PREP, split_rows, 0)
    on_diagonal = diagonal[...] != 0

    def build(group, carry):
        toeplitz[group, 35 * 128 : 36 * 128] = jnp.zeros((128, 256), BF16)
        for i in range(70):
            toeplitz[group, i * 64 : i * 64 + 64] = jnp.where(
                on_diagonal,
                jnp.broadcast_to(taps[group, i : i + 1, :], (64, 256)),
                jnp.zeros((), BF16),
            )
        return carry

    lax.fori_loop(0, 4, build, 0)

    def convolve(chunk, conv, group):
        first = chunk * CHUNK

        def half(n):
            n = min(n, 34)
            return blocks[group, n % 5, pl.ds(first + n // 5, CHUNK)].reshape(CHUNK * 48, 128)

        total = None
        for pair in range(18):
            piece = jnp.concatenate([half(2 * pair), half(2 * pair + 1)], axis=1)
            term = jnp.dot(
                piece, toeplitz[group, pair * 256 : pair * 256 + 256], preferred_element_type=F32
            )
            total = term if total is None else total + term
        conv[group] = total

    def normalise(chunk, conv, r):
        sums = [conv[group, r * 48 : r * 48 + 48] for group in range(4)]
        if forced:
            force = lax.dot_general(
                flux[chunk * CHUNK + r],
                mixing[...],
                (((0,), (0,)), ((), ())),
                preferred_element_type=F32,
            )
        for hh in range(2):
            parts = [[None, None], [None, None]]
            for h in range(2):
                a = sums[2 * h][:, 128 * hh : 128 * hh + 128]
                b = sums[2 * h + 1][:, 128 * hh : 128 * hh + 128]
                parts[0][h] = jnp.where(lower, a, pltpu.roll(b, 64, 1))
                parts[1][h] = jnp.where(lower, pltpu.roll(a, 64, 1), b)
            for parity in range(2):
                jo = 2 * hh + parity
                v0, v1 = parts[parity]
                mean = jnp.sum(v0 + v1, axis=-1, keepdims=True) * (1.0 / CHANNELS)
                c0 = v0 - mean
                c1 = v1 - mean
                var = jnp.sum(c0 * c0 + c1 * c1, axis=-1, keepdims=True) * (1.0 / CHANNELS)
                rs = lax.rsqrt(var + EPSILON)
                n0 = c0 * rs * gain[:, 0:128]
                n1 = c1 * rs * gain[:, 128:256]
                at = jo * 48
                if forced:
                    n0 = n0 + force[at : at + 48, :128]
                    n1 = n1 + force[at : at + 48, 128:]
                normed[r * 192 + at : r * 192 + at + 48, 0:128] = n0.astype(BF16)
                normed[r * 192 + at : r * 192 + at + 48, 128:256] = n1.astype(BF16)

    def mix(chunk):
        hidden = jnp.dot(normed[...], up[...], preferred_element_type=F32).astype(BF16)
        hidden = scaled_gelu(hidden).astype(BF16)
        branch = jnp.dot(hidden, down[...], preferred_element_type=F32)
        branch = (branch * (0.5 / GELU_SCALE)).astype(BF16)
        for r in range(CHUNK):
            row = chunk * CHUNK + r
            value = jnp.dot(
                spread[...], branch[r * 192 : r * 192 + 192], preferred_element_type=F32
            )
            value = value + x[row].astype(F32)
            keep = mask[row].astype(F32)
            out[row, :, 0:128] = (value[:, 0:128] * keep).astype(BF16)
            out[row, :, 128:256] = (value[:, 128:256] * keep).astype(BF16)

    def overlapped(chunk, conv, before, conv_before):
        done = 0
        for group in range(4):
            convolve(chunk, conv, group)
            while done * 4 < (group + 1) * CHUNK and done < CHUNK:
                normalise(before, conv_before, done)
                done += 1
        mix(before)

    buffers = (conv_a, conv_b)
    for group in range(4):
        convolve(0, conv_a, group)
    for chunk in range(1, chunks):
        overlapped(chunk, buffers[chunk % 2], chunk - 1, buffers[(chunk - 1) % 2])
    for r in range(CHUNK):
        normalise(chunks - 1, buffers[(chunks - 1) % 2], r)
    mix(chunks - 1)


def ocean_layer(x, top, bot, halo, taps, gain, up, down, mask, flux=None, mixing=None):
    gather, spread, diagonal = ocean_tables()
    forced = flux is not None
    args = [
        x,
        top,
        bot,
        halo,
        jnp.asarray(gather, BF16),
        expand_taps(taps),
        jnp.asarray(diagonal, BF16),
        gain[None] * GELU_SCALE,
        up,
        down,
        mask,
        jnp.asarray(spread, BF16),
    ]
    if forced:
        args += [flux, (mixing * GELU_SCALE).astype(BF16)]
    whole = pl.BlockSpec(memory_space=pltpu.VMEM)
    return pl.pallas_call(
        functools.partial(ocean_kernel, forced=forced),
        in_specs=[whole] * len(args),
        out_specs=whole,
        out_shape=jax.ShapeDtypeStruct((ROWS, COLS, CHANNELS), BF16),
        scratch_shapes=[
            pltpu.VMEM((PREP, 208, CHANNELS), BF16),
            pltpu.VMEM((4, 5, 36, 48, 128), BF16),
            pltpu.VMEM((4, 36 * 128, 256), BF16),
            pltpu.VMEM((4, CHUNK * 48, 256), F32),
            pltpu.VMEM((4, CHUNK * 48, 256), F32),
            pltpu.VMEM((CHUNK * 192, CHANNELS), BF16),
        ],
        compiler_params=pltpu.CompilerParams(vmem_limit_bytes=VMEM_BYTES),
        cost_estimate=pl.CostEstimate(
            flops=2 * 14_000_000_000, bytes_accessed=8_000_000, transcendentals=5_529_600
        ),
    )(*args)


def ring(axis, step, wrap):
    size = lax.axis_size(axis)
    pairs = [(i, i + step) for i in range(size)]
    if wrap:
        return [(i, j % size) for i, j in pairs]
    return [(i, j) for i, j in pairs if 0 <= j < size]


def halos(x):
    top = lax.ppermute(x[ROWS - 3 :], "row", ring("row", 1, False))
    bot = lax.ppermute(x[:3], "row", ring("row", -1, False))
    left = lax.ppermute(x[:, COLS - 3 :], "col", ring("col", 1, True))
    right = lax.ppermute(x[:, :3], "col", ring("col", -1, True))
    side = jnp.concatenate([left, right, jnp.zeros((ROWS, 10, CHANNELS), BF16)], 1)
    above = lax.ppermute(side[ROWS - 3 :], "row", ring("row", 1, False))
    below = lax.ppermute(side[:3], "row", ring("row", -1, False))
    return top, bot, jnp.concatenate([above, side, below], 0)


def body(
    sea_fields_now,
    water_site_flags,
    separable_stencils,
    sea_scaling_factors,
    sea_first_matrices,
    sea_second_matrices,
    exchange_to_sea_matrix,
    heat_emitter,
    air_fields_now,
    air_scaling_factors,
    harmonic_combine_matrix,
    air_first_matrix,
    air_second_matrix,
    exchange_emitter,
    heat_to_air_matrix,
    regrid_area_factors,
    link_regrid_group,
    patch_active_links,
):
    row_pos = lax.axis_index("row")
    col_pos = lax.axis_index("col")
    row_total = lax.axis_size("row")
    strip_meridian_number, strip_parallel_number, atmos_width = air_fields_now.shape
    tile_rows, tile_cols, ocean_channel_count = sea_fields_now.shape
    block_cells = strip_meridian_number // REGRID_GROUPS * strip_parallel_number
    block_total = row_total * REGRID_GROUPS
    lat_total = strip_parallel_number * row_total
    flux_cells = jnp.dot(
        air_fields_now.reshape(-1, atmos_width),
        exchange_emitter,
        preferred_element_type=jnp.float32,
    ).astype(jnp.bfloat16)
    flux_blocks = flux_cells.reshape(REGRID_GROUPS, block_cells, NF).transpose(0, 2, 1)
    heat_site_values = jnp.dot(
        sea_fields_now.reshape(-1, ocean_channel_count),
        heat_emitter,
        preferred_element_type=jnp.float32,
    )
    heat_site_values = (heat_site_values * water_site_flags.reshape(-1).astype(jnp.float32)).astype(
        jnp.bfloat16
    )
    column_pairs = link_regrid_group[:, 0, :]
    column_counts = patch_active_links[:, 0]
    own_pairs = lax.dynamic_index_in_dim(column_pairs, row_pos, 0, keepdims=False)
    own_count = lax.dynamic_index_in_dim(column_counts, row_pos, 0, keepdims=False)
    pair_slots = jnp.arange(PATCH_LINK_ROOM, dtype=jnp.int32)
    link_active_flag = pair_slots < own_count
    own_link_factors = regrid_area_factors[0, 0]
    link_heat_values = jnp.einsum(
        "hnc,c->hn", own_link_factors, heat_site_values, preferred_element_type=jnp.float32
    )
    link_heat_values = (link_heat_values * link_active_flag[:, None].astype(jnp.float32)).astype(
        jnp.bfloat16
    )
    parcel = jnp.concatenate(
        [flux_blocks, link_heat_values[:, None, :], jnp.zeros((3, 39, block_cells), BF16)], 1
    )
    parcel = jnp.pad(parcel, ((0, 0), (0, 0), (0, 256 - block_cells)))
    gathered = lax.all_gather(parcel, "row", axis=0, tiled=True)
    pick_pairs = (
        link_active_flag[:, None]
        & (own_pairs[:, None] == jnp.arange(block_total, dtype=jnp.int32)[None, :])
    ).astype(BF16)
    chosen = jnp.einsum(
        "pq,qfa->pfa", pick_pairs, gathered[:, :NF, :block_cells], preferred_element_type=F32
    )
    own_blocks = row_pos * REGRID_GROUPS + jnp.arange(REGRID_GROUPS, dtype=jnp.int32)
    landing = (own_blocks[:, None] == column_pairs.reshape(1, -1)).astype(BF16)
    own_heat_values = jnp.dot(
        landing, gathered[:, NF, :block_cells], preferred_element_type=F32
    )
    sea_exchange_values = jnp.einsum(
        "pfa,pao->fo",
        chosen.astype(BF16),
        own_link_factors,
        preferred_element_type=F32,
    )
    flux_rows = sea_exchange_values.astype(BF16).reshape(NF, ROWS, COLS)
    flux_rows = jnp.pad(flux_rows, ((0, 0), (0, 0), (0, 12))).reshape(NF, ROWS, 48, 4)
    flux_rows = flux_rows.transpose(1, 0, 3, 2).reshape(ROWS, NF, 192)
    zonal_basis = zonal_table(MERIDIAN_TOTAL, MMAX)
    merid_basis = merid_table(lat_total, LMODES)
    zonal_own = lax.dynamic_slice_in_dim(
        zonal_basis, col_pos * strip_meridian_number, strip_meridian_number, 0
    )
    merid_own = lax.dynamic_slice_in_dim(
        merid_basis, row_pos * strip_parallel_number, strip_parallel_number, 0
    )
    state_f = air_fields_now.astype(jnp.float32)
    normed = rescale_features(state_f, air_scaling_factors[0]).astype(jnp.bfloat16)
    basis_piece = zonal_own
    zonal_coeffs = lax.psum_scatter(
        jnp.einsum("ok,otc->ktc", basis_piece, normed, preferred_element_type=jnp.float32).astype(
            jnp.bfloat16
        ),
        "col",
        scatter_dimension=0,
        tiled=True,
    )
    basis_piece = merid_own
    spectra = lax.psum_scatter(
        jnp.einsum(
            "tl,ktc->lkc", basis_piece, zonal_coeffs, preferred_element_type=jnp.float32
        ).astype(jnp.bfloat16),
        "row",
        scatter_dimension=0,
        tiled=True,
    )
    filtered = jnp.einsum(
        "lkc,lcd->lkd", spectra, harmonic_combine_matrix, preferred_element_type=jnp.float32
    ).astype(jnp.bfloat16)
    basis_piece = merid_own
    band_coeffs = jnp.einsum(
        "tl,lkc->tkc",
        basis_piece,
        lax.all_gather(filtered, "row", axis=0, tiled=True),
        preferred_element_type=jnp.float32,
    ).astype(jnp.bfloat16)
    basis_piece = zonal_own
    spectral_out = jnp.einsum(
        "ok,tkc->otc",
        basis_piece,
        lax.all_gather(band_coeffs, "col", axis=1, tiled=True),
        preferred_element_type=jnp.float32,
    )
    air_fields_hidden = state_f + spectral_out
    heat_lattice = own_heat_values.reshape(strip_meridian_number, strip_parallel_number)
    air_fields_entry = (
        rescale_features(air_fields_hidden, air_scaling_factors[1])
        + heat_lattice[..., None] * heat_to_air_matrix
    )
    air_fields_entry = air_fields_entry.astype(jnp.bfloat16).reshape(-1, atmos_width)
    atmos_hidden = jax.nn.gelu(
        jnp.dot(air_fields_entry, air_first_matrix, preferred_element_type=jnp.float32),
        approximate=True,
    ).astype(jnp.bfloat16)
    atmos_result = air_fields_hidden.reshape(-1, atmos_width) + jnp.dot(
        atmos_hidden, air_second_matrix, preferred_element_type=jnp.float32
    )
    air_fields_next = atmos_result.reshape(
        strip_meridian_number, strip_parallel_number, atmos_width
    ).astype(jnp.bfloat16)
    mask = jnp.broadcast_to(water_site_flags[..., None], (ROWS, COLS, 128)).astype(BF16)
    current = sea_fields_now
    for layer in range(LAYERS):
        top, bot, side = halos(current)
        extra = (flux_rows, exchange_to_sea_matrix) if layer == LAYERS - 1 else ()
        current = ocean_layer(
            current,
            top,
            bot,
            side,
            separable_stencils[layer],
            sea_scaling_factors[layer],
            sea_first_matrices[layer],
            sea_second_matrices[layer],
            mask,
            *extra,
        )
    return (current, air_fields_next)


def solution(mesh):
    in_specs = (
        P("row", "col", None),
        P("row", "col"),
        P(),
        P(),
        P(),
        P(),
        P(),
        P(),
        P("col", "row", None),
        P(),
        P("row", None, None),
        P(),
        P(),
        P(),
        P(),
        P("row", "col", None, None, None),
        P(None, "col", None),
        P(None, "col"),
    )
    out_specs = (P("row", "col", None), P("col", "row", None))
    return jax.shard_map(body, mesh=mesh, in_specs=in_specs, out_specs=out_specs, check_vma=False)
```

```python
import functools
import math

import jax
import jax.numpy as jnp
import numpy as np
from jax import lax
from jax.experimental import pallas as pl
from jax.experimental.pallas import tpu as pltpu
from jax.sharding import PartitionSpec as P

NF = 8
MERIDIAN_TOTAL = 360
MMAX = 96
LMODES = 96
LAYERS = 2
REGRID_GROUPS = 3
PATCH_LINK_ROOM = 3


EPSILON = 1e-06
HIGHEST_MODE = lax.Precision.HIGHEST


BF16 = jnp.bfloat16
F32 = jnp.float32
GELU_SLOPE = math.sqrt(2.0 / math.pi)
GELU_SCALE = (GELU_SLOPE * 0.044715) ** (1.0 / 3.0)
GELU_LINEAR = GELU_SLOPE / GELU_SCALE
VMEM_BYTES = 60 * 1024 * 1024
ROWS = 30
COLS = 180
CHANNELS = 256
PREP = 6


def scaled_gelu(scaled):
    inner = (scaled * scaled + GELU_LINEAR) * scaled
    return scaled + scaled * jnp.tanh(inner)


def ocean_tables(wide):
    reach = 6 if wide else 0
    width = 208 if wide else 192
    gather = np.zeros((480, width), np.float32)
    for shift in range(10):
        for block in range(48):
            place = 4 * block + shift - reach
            if wide and -6 <= place < 0:
                place = 192 + place + 6
            elif wide and COLS <= place < COLS + 6:
                place = 198 + place - COLS
            elif not 0 <= place < (COLS if wide else COLS + 6):
                continue
            gather[shift * 48 + block, place] = 1
    cells = 192 if wide else COLS
    spread = np.zeros((cells, 192), np.float32)
    for place in range(cells):
        spread[place, (place % 4) * 48 + place // 4] = 1
    shift = np.zeros((192, 208), np.float32)
    for cell in range(-3, COLS + 3):
        source = 192 + cell + 6 if cell < 0 else 198 + cell - COLS if cell >= COLS else cell
        shift[cell + 3, source] = 1
    diagonal = np.tile(np.eye(64, dtype=np.float32), (1, 4))
    return gather, spread, diagonal, shift


def expand_taps(taps):
    empty = jnp.zeros((7, CHANNELS), taps.dtype)
    offsets = []
    for offset in range(10):
        offsets.append(
            jnp.stack([taps[:, offset - out] if 0 <= offset - out < 7 else empty for out in range(4)], 1)
        )
    table = jnp.stack(offsets, 1)
    return table.reshape(70, 4, 4, 64).transpose(2, 0, 1, 3).reshape(4, 70, 256)


def ocean_kernel(*refs, wide):
    gather, taps, diagonal, gain, up, down, mask, spread, x = refs[:9]
    if wide:
        top, bot, side, above, below, shift = refs[9:15]
        out, blocks, toeplitz, conv_a, conv_b, normed, kept, line, flags = refs[15:]
    else:
        flux, mixing, out, blocks, toeplitz, conv_a, conv_b, normed, kept = refs[9:]
    rows = ROWS + 6 if wide else ROWS
    chunk_rows = rows // 3
    chunks = 3
    lower = lax.broadcasted_iota(jnp.int32, (48, 128), 1) < 64

    def split_row(cells, row):
        moved = jnp.dot(gather[...], cells, preferred_element_type=F32)
        for k in range(5):
            even = moved[96 * k : 96 * k + 48]
            odd = moved[96 * k + 48 : 96 * k + 96]
            for h in range(2):
                e = even[:, 128 * h : 128 * h + 128]
                o = odd[:, 128 * h : 128 * h + 128]
                blocks[2 * h, k, row] = jnp.where(lower, e, pltpu.roll(o, 64, 1)).astype(BF16)
                blocks[2 * h + 1, k, row] = jnp.where(lower, pltpu.roll(e, 64, 1), o).astype(BF16)
        return moved[144:336].astype(BF16)

    def wide_row(cells, halo, row, slot):
        line[slot, 0:180] = cells
        line[slot, 192:208] = halo
        return split_row(line[slot], row)

    if wide:
        for slot in range(PREP):
            line[slot, 176:192] = jnp.zeros((16, CHANNELS), BF16)
        for q in range(6):
            own = wide_row(top[q], above[q], q, q)
            if q >= 3:
                kept[q - 3] = own

        def split_rows(step, carry):
            for q in range(PREP):
                at = PREP * step + q
                kept[at + 3] = wide_row(x[at], side[at], at + 6, q)
            return carry

        lax.fori_loop(0, ROWS // PREP, split_rows, 0)
        for q in range(6):
            own = wide_row(bot[q], below[q], 36 + q, q)
            if q < 3:
                kept[33 + q] = own
        flags[176:192] = jnp.zeros((16, 128), F32)
        flags[0:180] = mask[...] + top[6, :, 0:128].astype(F32) + bot[6, :, 0:128].astype(F32)
        flags[192:208] = (
            side[30, :, 0:128].astype(F32)
            + above[6, :, 0:128].astype(F32)
            + below[6, :, 0:128].astype(F32)
        )
        keep_all = jnp.dot(shift[...], flags[...].astype(BF16), preferred_element_type=F32)
    else:

        def split_rows(step, carry):
            for q in range(PREP):
                at = PREP * step + q
                own = split_row(x[at], at)
                kept[jnp.clip(at - 3, 0, ROWS - 1)] = own
            return carry

        lax.fori_loop(0, 6, split_rows, 0)
        kept[ROWS - 1] = jnp.dot(
            gather[144:336, :], x[ROWS + 2], preferred_element_type=F32
        ).astype(BF16)
        keep_all = mask[...]
    on_diagonal = diagonal[...] != 0

    def build(group, carry):
        toeplitz[group, 35 * 128 : 36 * 128] = jnp.zeros((128, 256), BF16)
        for i in range(70):
            toeplitz[group, i * 64 : i * 64 + 64] = jnp.where(
                on_diagonal,
                jnp.broadcast_to(taps[group, i : i + 1, :], (64, 256)),
                jnp.zeros((), BF16),
            )
        return carry

    lax.fori_loop(0, 4, build, 0)

    def convolve(chunk, conv, group):
        first = chunk * chunk_rows

        def half(n):
            n = min(n, 34)
            return blocks[group, n % 5, pl.ds(first + n // 5, chunk_rows)].reshape(chunk_rows * 48, 128)

        total = None
        for pair in range(18):
            piece = jnp.concatenate([half(2 * pair), half(2 * pair + 1)], axis=1)
            term = jnp.dot(
                piece, toeplitz[group, pair * 256 : pair * 256 + 256], preferred_element_type=F32
            )
            total = term if total is None else total + term
        conv[group] = total

    def normalise(chunk, conv, r):
        sums = [conv[group, r * 48 : r * 48 + 48] for group in range(4)]
        if not wide:
            force = lax.dot_general(
                flux[chunk * chunk_rows + r],
                mixing[...],
                (((0,), (0,)), ((), ())),
                preferred_element_type=F32,
            )
        for hh in range(2):
            parts = [[None, None], [None, None]]
            for h in range(2):
                a = sums[2 * h][:, 128 * hh : 128 * hh + 128]
                b = sums[2 * h + 1][:, 128 * hh : 128 * hh + 128]
                parts[0][h] = jnp.where(lower, a, pltpu.roll(b, 64, 1))
                parts[1][h] = jnp.where(lower, pltpu.roll(a, 64, 1), b)
            for parity in range(2):
                jo = 2 * hh + parity
                v0, v1 = parts[parity]
                mean = jnp.sum(v0 + v1, axis=-1, keepdims=True) * (1.0 / CHANNELS)
                c0 = v0 - mean
                c1 = v1 - mean
                var = jnp.sum(c0 * c0 + c1 * c1, axis=-1, keepdims=True) * (1.0 / CHANNELS)
                rs = lax.rsqrt(var + EPSILON)
                n0 = c0 * rs * gain[:, 0:128]
                n1 = c1 * rs * gain[:, 128:256]
                at = jo * 48
                if not wide:
                    n0 = n0 + force[at : at + 48, :128]
                    n1 = n1 + force[at : at + 48, 128:]
                normed[r * 192 + at : r * 192 + at + 48, 0:128] = n0.astype(BF16)
                normed[r * 192 + at : r * 192 + at + 48, 128:256] = n1.astype(BF16)

    def mix(chunk):
        hidden = jnp.dot(normed[...], up[...], preferred_element_type=F32).astype(BF16)
        hidden = scaled_gelu(hidden).astype(BF16)
        branch = jnp.dot(hidden, down[...], preferred_element_type=F32)
        branch = branch * (0.5 / GELU_SCALE)
        for r in range(chunk_rows):
            row = chunk * chunk_rows + r
            value = (branch[r * 192 : r * 192 + 192] + kept[row].astype(F32)).astype(BF16)
            value = jnp.dot(spread[...], value, preferred_element_type=F32)
            keep = keep_all[:, 3 * (not wide) + row : 3 * (not wide) + row + 1]
            out[row] = (value * keep).astype(BF16)

    def overlapped(chunk, conv, before, conv_before):
        done = 0
        for group in range(4):
            convolve(chunk, conv, group)
            while done * 4 < (group + 1) * chunk_rows and done < chunk_rows:
                normalise(before, conv_before, done)
                done += 1
        mix(before)

    buffers = (conv_a, conv_b)
    for group in range(4):
        convolve(0, conv_a, group)
    for chunk in range(1, chunks):
        overlapped(chunk, buffers[chunk % 2], chunk - 1, buffers[(chunk - 1) % 2])
    for r in range(chunk_rows):
        normalise(chunks - 1, buffers[(chunks - 1) % 2], r)
    mix(chunks - 1)


def ocean_layer(x, taps, gain, up, down, mask, halo=None, flux=None, mixing=None):
    wide = halo is not None
    gather, spread, diagonal, shift = ocean_tables(wide)
    rows = ROWS + 6 if wide else ROWS
    args = [
        jnp.asarray(gather, BF16),
        expand_taps(taps),
        jnp.asarray(diagonal, BF16),
        gain[None] * GELU_SCALE,
        up,
        down,
        mask,
        jnp.asarray(spread, BF16),
        x,
    ]
    scratch = [
        pltpu.VMEM((4, 5, rows + 6, 48, 128), BF16),
        pltpu.VMEM((4, 36 * 128, 256), BF16),
        pltpu.VMEM((4, rows * 16, 256), F32),
        pltpu.VMEM((4, rows * 16, 256), F32),
        pltpu.VMEM((rows * 64, CHANNELS), BF16),
        pltpu.VMEM((rows, 192, CHANNELS), BF16),
    ]
    if wide:
        args += [*halo, jnp.asarray(shift, BF16)]
        scratch += [pltpu.VMEM((PREP, 208, CHANNELS), BF16), pltpu.VMEM((208, 128), F32)]
    else:
        args += [flux, (mixing * GELU_SCALE).astype(BF16)]
    whole = pl.BlockSpec(memory_space=pltpu.VMEM)
    return pl.pallas_call(
        functools.partial(ocean_kernel, wide=wide),
        in_specs=[whole] * len(args),
        out_specs=whole,
        out_shape=jax.ShapeDtypeStruct((rows, 192 if wide else COLS, CHANNELS), BF16),
        scratch_shapes=scratch,
        compiler_params=pltpu.CompilerParams(vmem_limit_bytes=VMEM_BYTES),
        cost_estimate=pl.CostEstimate(
            flops=2 * 14_000_000_000, bytes_accessed=8_000_000, transcendentals=5_529_600
        ),
    )(*args)


def ring(axis, step, wrap):
    size = lax.axis_size(axis)
    pairs = [(i, i + step) for i in range(size)]
    if wrap:
        return [(i, j % size) for i, j in pairs]
    return [(i, j) for i, j in pairs if 0 <= j < size]


def lanes_at(columns, first):
    return jnp.pad(columns, ((0, 0), (first, CHANNELS - first - columns.shape[1])))[None]


def halos(x, flags):
    over = jnp.concatenate([x[ROWS - 6 :], lanes_at(flags[ROWS - 3 :].T, 0)], 0)
    under = jnp.concatenate([x[:6], lanes_at(flags[:3].T, 33)], 0)
    turned = lanes_at(flags.T, 3)
    top = lax.ppermute(over, "row", ring("row", 1, False))
    bot = lax.ppermute(under, "row", ring("row", -1, False))
    east = jnp.concatenate([x[:, COLS - 6 :], turned[:, COLS - 6 :]], 0)
    west = jnp.concatenate([x[:, :6], turned[:, :6]], 0)
    left = lax.ppermute(east, "col", ring("col", 1, True))
    right = lax.ppermute(west, "col", ring("col", -1, True))
    side = jnp.concatenate([left, right, jnp.zeros((ROWS + 1, 4, CHANNELS), BF16)], 1)
    corner = jnp.concatenate([side[ROWS - 6 : ROWS], lanes_at(side[ROWS, :, 30:33], 0)], 0)
    above = lax.ppermute(corner, "row", ring("row", 1, False))
    corner = jnp.concatenate([side[:6], lanes_at(side[ROWS, :, 3:6], 33)], 0)
    below = lax.ppermute(corner, "row", ring("row", -1, False))
    mask = turned[0, :, :128].astype(F32)
    return mask, (top, bot, side, above, below)


AIR = 384
SPAN_LON = 45
SPAN_LAT = 12
WAVES = 192


def spectral_tables():
    lon = np.arange(360)
    wave = np.arange(WAVES)
    angle = 2.0 * np.pi / 360 * (lon[:, None] * (wave[None, :] % MMAX) % 360)
    zonal = np.where(wave[None, :] < MMAX, np.cos(angle), np.sin(angle)) * math.sqrt(2.0 / 360)
    lat = np.arange(192)
    mode = np.arange(LMODES)
    angle = np.pi / 384 * ((2 * lat[:, None] + 1) * mode[None, :] % 768)
    merid = np.cos(angle) * math.sqrt(2.0 / 192)
    zonal = zonal.astype(np.float32).astype(BF16).astype(np.float32)
    merid = merid.astype(np.float32).astype(BF16).astype(np.float32)
    zf = np.zeros((8, 128, 384), np.float32)
    for q in range(8):
        for t2 in range(2):
            zf[q, t2 * 48 : t2 * 48 + 45, t2 * 192 : t2 * 192 + 192] = zonal[q * 45 : q * 45 + 45]
    mf = np.zeros((3, 2, 16, 8, 16, 8, 3), np.float32)
    by_band = merid.reshape(16, 6, 2, 16, 6)
    for c in range(3):
        for t2 in range(2):
            mf[c, t2, :, :6, :, :6, c] = by_band[:, :, t2].transpose(2, 3, 0, 1)
    place = np.zeros((3, 192, 8, 128), np.float32)
    for c in range(3):
        for q in range(8):
            for k in range(24):
                place[c, q * 24 + k, q, c * 24 + k] = 1
    mi = np.zeros((2, 16, 8, 16, 8), np.float32)
    mi[:, :, :6, :, :6] = by_band.transpose(2, 0, 1, 3, 4)
    zi = np.zeros((8, 3, 128, 8, 48), np.float32)
    for q in range(8):
        for c in range(3):
            zi[q, c, c * 24 : c * 24 + 24, :, :45] = (
                zonal[:, q * 24 : q * 24 + 24].reshape(8, 45, 24).transpose(2, 0, 1)
            )
    return (
        zf,
        mf.reshape(3, 2, 128, 384),
        place.reshape(3, 192, 1024),
        mi.reshape(256, 128),
        zi.reshape(8, 3, 128, 384),
    )


def feature_norm(values, gain_row):
    centred = values - jnp.sum(values, axis=-1, keepdims=True) * (1.0 / AIR)
    spread_sq = jnp.sum(centred * centred, axis=-1, keepdims=True) * (1.0 / AIR)
    return centred * lax.rsqrt(spread_sq + EPSILON) * gain_row


def flatten_air(air, flat):
    for c in range(3):
        for i in range(SPAN_LON):
            flat[c, 12 * i : 12 * i + 12] = air[i, :, 128 * c : 128 * c + 128].astype(F32)
        flat[c, 540:] = jnp.zeros((36, 128), F32)


def latitude(flat, t):
    return jnp.concatenate([flat[c, pl.ds(t, 48, stride=12)] for c in range(3)], axis=1)


def air_send_kernel(air, gain, emitter, flux_out, send, flat, work):
    flatten_air(air, flat)
    flux = lax.dot_general(
        emitter[...],
        jnp.concatenate([flat[c, 0:540] for c in range(3)], axis=1).astype(BF16),
        (((1,), (1,)), ((), ())),
        preferred_element_type=F32,
    )
    for block in range(3):
        flux_out[block] = flux[:, block * 180 : block * 180 + 180].astype(BF16)
    zeros = jnp.zeros((32, AIR), F32)
    for t6 in range(6):
        pieces = []
        for t2 in range(2):
            pieces.append(feature_norm(latitude(flat, 2 * t6 + t2), gain[...]))
        pair = jnp.concatenate(pieces + [zeros], axis=0)
        for c in range(3):
            work[pl.ds(t6 * 3 + c, 128, stride=24)] = pair[:, c * 128 : c * 128 + 128].T
    for r in range(18, 24):
        work[pl.ds(r, 128, stride=24)] = jnp.zeros((128, 128), F32)

    def pack(step, carry):
        at = pl.multiple_of(step * 8, 8)
        block = work[pl.ds(pl.multiple_of(step * 192, 192), 192)]
        send[pl.ds(at, 8)] = block.reshape(8, 24, 128).astype(BF16)
        return carry

    lax.fori_loop(0, 16, pack, 0)


def forward_kernel(got, zf, mf, place, send):
    total = None
    for q in range(8):
        part = got[:, q].astype(F32).reshape(384, 128).astype(BF16)
        term = jnp.dot(part, zf[q], preferred_element_type=F32)
        total = term if total is None else total + term
    total = total.astype(BF16)
    moved = None
    for c in range(3):
        modes = None
        for t2 in range(2):
            term = jnp.dot(
                mf[c, t2], total[:, t2 * 192 : t2 * 192 + 192], preferred_element_type=F32
            )
            modes = term if modes is None else modes + term
        term = jnp.dot(modes.astype(BF16), place[c], preferred_element_type=F32)
        moved = term if moved is None else moved + term
    for r in range(16):
        for q in range(8):
            send[r * 8 + q] = moved[8 * r : 8 * r + 8, 128 * q : 128 * q + 128].astype(BF16)


def filter_kernel(got, mixing, send, work):
    work[...] = got[...].astype(F32).reshape(1024, 128)
    zeros = jnp.zeros((56, 128), F32)
    results = []
    for mode in range(6):
        turned = work[pl.ds(mode, 128, stride=8)].T
        lhs = jnp.concatenate([turned[24 * c : 24 * c + 24] for c in range(3)], axis=1)
        result = jnp.dot(lhs.astype(BF16), mixing[mode], preferred_element_type=F32)
        stacked = [result[:, 128 * c : 128 * c + 128] for c in range(3)]
        results.append(jnp.concatenate(stacked + [zeros], axis=0).T)
    for mode in range(6):
        work[pl.ds(mode, 128, stride=8)] = results[mode]
    for mode in range(6, 8):
        work[pl.ds(mode, 128, stride=8)] = jnp.zeros((128, 128), F32)
    send[...] = work[...].reshape(128, 8, 128).astype(BF16)


def inverse_kernel(got, mi, zi, send):
    totals = [None, None, None]
    for q in range(8):
        part = got[:, q].astype(F32).reshape(128, 128).astype(BF16)
        bands = jnp.dot(mi[...], part, preferred_element_type=F32).astype(BF16)
        for c in range(3):
            term = jnp.dot(bands, zi[q, c], preferred_element_type=F32)
            totals[c] = term if totals[c] is None else totals[c] + term
    zeros = jnp.zeros((8, 32), F32)
    for c in range(3):
        for r in range(16):
            first = totals[c][8 * r : 8 * r + 8]
            second = totals[c][128 + 8 * r : 128 + 8 * r + 8]
            for q in range(8):
                row = jnp.concatenate(
                    [first[:, 48 * q : 48 * q + 48], second[:, 48 * q : 48 * q + 48], zeros], axis=1
                )
                send[r * 8 + q, 8 * c : 8 * c + 8] = row.astype(BF16)


def air_finish_kernel(got, air, gain, sst, heat, up, down, out, work, flat, mid):
    work[...] = got[...].astype(F32).reshape(128 * 24, 128)
    flatten_air(air, flat)
    entries = []
    for t6 in range(6):
        turned = [work[pl.ds(8 * c + t6, 128, stride=24)].T for c in range(3)]
        for t2 in range(2):
            t = 2 * t6 + t2
            spectral = jnp.concatenate([v[48 * t2 : 48 * t2 + 48] for v in turned], axis=1)
            value = latitude(flat, t) + spectral
            mid[48 * t : 48 * t + 48] = value
            entry = feature_norm(value, gain[...]) + sst[:, t : t + 1] * heat[...]
            entries.append(entry.astype(BF16))
    entry = jnp.concatenate(entries, axis=0)
    hidden = jnp.dot(entry, up[...], preferred_element_type=F32)
    hidden = jax.nn.gelu(hidden, approximate=True).astype(BF16)
    result = mid[...] + jnp.dot(hidden, down[...], preferred_element_type=F32)
    for t in range(SPAN_LAT):
        for c in range(3):
            flat[c, pl.ds(t, 48, stride=12)] = result[48 * t : 48 * t + 48, 128 * c : 128 * c + 128]
    for i in range(SPAN_LON):
        for c in range(3):
            out[i, :, 128 * c : 128 * c + 128] = flat[c, 12 * i : 12 * i + 12].astype(BF16)


def plain_kernel(kernel, outs, scratch, flops, *args):
    whole = pl.BlockSpec(memory_space=pltpu.VMEM)
    size = sum(math.prod(a.shape) * a.dtype.itemsize for a in args)
    return pl.pallas_call(
        kernel,
        in_specs=[whole] * len(args),
        out_specs=[whole] * len(outs),
        out_shape=[jax.ShapeDtypeStruct(s, BF16) for s in outs],
        scratch_shapes=[pltpu.VMEM(s, F32) for s in scratch],
        compiler_params=pltpu.CompilerParams(vmem_limit_bytes=VMEM_BYTES),
        cost_estimate=pl.CostEstimate(flops=flops, bytes_accessed=size, transcendentals=0),
    )(*args)


def swap(message):
    return lax.all_to_all(message, ("row", "col"), 0, 0, tiled=True)


def spectral_chain(message, harmonic):
    zf, mf, place, mi, zi = [jnp.asarray(t, BF16) for t in spectral_tables()]
    got = swap(message).reshape(16, 8, 24, 128)
    (message,) = plain_kernel(
        forward_kernel, [(128, 8, 128)], [], 2_000_000_000, got, zf, mf, place
    )
    got = swap(message)
    (message,) = plain_kernel(
        filter_kernel, [(128, 8, 128)], [(1024, 128)], 500_000_000, got, harmonic
    )
    got = swap(message).reshape(16, 8, 8, 128)
    (message,) = plain_kernel(inverse_kernel, [(128, 24, 128)], [], 2_000_000_000, got, mi, zi)
    return swap(message)


def body(
    sea_fields_now,
    water_site_flags,
    separable_stencils,
    sea_scaling_factors,
    sea_first_matrices,
    sea_second_matrices,
    exchange_to_sea_matrix,
    heat_emitter,
    air_fields_now,
    air_scaling_factors,
    harmonic_combine_matrix,
    air_first_matrix,
    air_second_matrix,
    exchange_emitter,
    heat_to_air_matrix,
    regrid_area_factors,
    link_regrid_group,
    patch_active_links,
):
    row_pos = lax.axis_index("row")
    col_pos = lax.axis_index("col")
    row_total = lax.axis_size("row")
    strip_meridian_number, strip_parallel_number, atmos_width = air_fields_now.shape
    tile_rows, tile_cols, ocean_channel_count = sea_fields_now.shape
    block_cells = strip_meridian_number // REGRID_GROUPS * strip_parallel_number
    block_total = row_total * REGRID_GROUPS
    flux_blocks, message = plain_kernel(
        air_send_kernel,
        [(3, NF, 180), (128, 24, 128)],
        [(3, 576, 128), (3072, 128)],
        100_000_000,
        air_fields_now,
        air_scaling_factors[0:1],
        exchange_emitter.T,
    )
    heat_site_values = jnp.einsum(
        "yxc,c->yx", sea_fields_now, heat_emitter, preferred_element_type=F32
    )
    heat_site_values = (heat_site_values * water_site_flags.astype(F32)).astype(BF16).reshape(-1)
    column_pairs = link_regrid_group[:, 0, :]
    column_counts = patch_active_links[:, 0]
    own_pairs = lax.dynamic_index_in_dim(column_pairs, row_pos, 0, keepdims=False)
    own_count = lax.dynamic_index_in_dim(column_counts, row_pos, 0, keepdims=False)
    pair_slots = jnp.arange(PATCH_LINK_ROOM, dtype=jnp.int32)
    link_active_flag = pair_slots < own_count
    own_link_factors = regrid_area_factors[0, 0]
    link_heat_values = jnp.einsum(
        "hnc,c->hn", own_link_factors, heat_site_values, preferred_element_type=jnp.float32
    )
    link_heat_values = (link_heat_values * link_active_flag[:, None].astype(jnp.float32)).astype(
        jnp.bfloat16
    )
    parcel = jnp.concatenate(
        [flux_blocks, link_heat_values[:, None, :], jnp.zeros((3, 39, block_cells), BF16)], 1
    )
    parcel = jnp.pad(parcel, ((0, 0), (0, 0), (0, 256 - block_cells)))
    gathered = lax.all_gather(parcel, "row", axis=0, tiled=True)
    pick_pairs = (
        link_active_flag[:, None]
        & (own_pairs[:, None] == jnp.arange(block_total, dtype=jnp.int32)[None, :])
    ).astype(BF16)
    chosen = jnp.einsum(
        "pq,qfa->pfa", pick_pairs, gathered[:, :NF, :block_cells], preferred_element_type=F32
    )
    own_blocks = row_pos * REGRID_GROUPS + jnp.arange(REGRID_GROUPS, dtype=jnp.int32)
    landing = (own_blocks[:, None] == column_pairs.reshape(1, -1)).astype(BF16)
    own_heat_values = jnp.dot(
        landing, gathered[:, NF, :block_cells], preferred_element_type=F32
    )
    sea_exchange_values = jnp.einsum(
        "pfa,pao->fo",
        chosen.astype(BF16),
        own_link_factors,
        preferred_element_type=F32,
    )
    flux_rows = sea_exchange_values.astype(BF16).reshape(NF, ROWS, COLS)
    flux_rows = jnp.pad(flux_rows, ((0, 0), (0, 0), (0, 12))).reshape(NF, ROWS, 48, 4)
    flux_rows = flux_rows.transpose(1, 0, 3, 2).reshape(ROWS, NF, 192)
    heat_lattice = jnp.pad(
        own_heat_values.reshape(strip_meridian_number, strip_parallel_number), ((0, 3), (0, 0))
    )
    spectral = spectral_chain(message, harmonic_combine_matrix)
    (air_fields_next,) = plain_kernel(
        air_finish_kernel,
        [air_fields_now.shape],
        [(3072, 128), (3, 576, 128), (576, AIR)],
        700_000_000,
        spectral,
        air_fields_now,
        air_scaling_factors[1:2],
        heat_lattice,
        heat_to_air_matrix[None],
        air_first_matrix,
        air_second_matrix,
    )
    mask, halo = halos(sea_fields_now, water_site_flags.astype(BF16))
    layers = []
    for layer in range(LAYERS):
        layers.append(
            (
                separable_stencils[layer],
                sea_scaling_factors[layer],
                sea_first_matrices[layer],
                sea_second_matrices[layer],
                mask,
            )
        )
    current = ocean_layer(sea_fields_now, *layers[0], halo=halo)
    current = ocean_layer(current, *layers[1], flux=flux_rows, mixing=exchange_to_sea_matrix)
    return (current, air_fields_next)


def solution(mesh):
    in_specs = (
        P("row", "col", None),
        P("row", "col"),
        P(),
        P(),
        P(),
        P(),
        P(),
        P(),
        P("col", "row", None),
        P(),
        P("row", None, None),
        P(),
        P(),
        P(),
        P(),
        P("row", "col", None, None, None),
        P(None, "col", None),
        P(None, "col"),
    )
    out_specs = (P("row", "col", None), P("col", "row", None))
    return jax.shard_map(body, mesh=mesh, in_specs=in_specs, out_specs=out_specs, check_vma=False)
```

```python
import functools
import math

import jax
import jax.numpy as jnp
import numpy as np
from jax import lax
from jax.experimental import pallas as pl
from jax.experimental.pallas import tpu as pltpu
from jax.sharding import PartitionSpec as P

NF = 8
MERIDIAN_TOTAL = 360
MMAX = 96
LMODES = 96
LAYERS = 2
REGRID_GROUPS = 3
PATCH_LINK_ROOM = 3


EPSILON = 1e-06
HIGHEST_MODE = lax.Precision.HIGHEST


BF16 = jnp.bfloat16
F32 = jnp.float32
GELU_SLOPE = math.sqrt(2.0 / math.pi)
GELU_SCALE = (GELU_SLOPE * 0.044715) ** (1.0 / 3.0)
GELU_LINEAR = GELU_SLOPE / GELU_SCALE
VMEM_BYTES = 60 * 1024 * 1024
ROWS = 30
COLS = 180
CHANNELS = 256
PREP = 6


def scaled_gelu(scaled):
    inner = (scaled * scaled + GELU_LINEAR) * scaled
    return scaled + scaled * jnp.tanh(inner)


def ocean_tables(wide):
    reach = 6 if wide else 0
    width = 208 if wide else 192
    gather = np.zeros((480, width), np.float32)
    for shift in range(10):
        for block in range(48):
            place = 4 * block + shift - reach
            if wide and -6 <= place < 0:
                place = 192 + place + 6
            elif wide and COLS <= place < COLS + 6:
                place = 198 + place - COLS
            elif not 0 <= place < (COLS if wide else COLS + 6):
                continue
            gather[shift * 48 + block, place] = 1
    cells = 192 if wide else COLS
    spread = np.zeros((cells, 192), np.float32)
    for place in range(cells):
        spread[place, (place % 4) * 48 + place // 4] = 1
    shift = np.zeros((192, 208), np.float32)
    for cell in range(-3, COLS + 3):
        source = 192 + cell + 6 if cell < 0 else 198 + cell - COLS if cell >= COLS else cell
        shift[cell + 3, source] = 1
    diagonal = np.tile(np.eye(64, dtype=np.float32), (1, 4))
    return gather, spread, diagonal, shift


def expand_taps(taps):
    empty = jnp.zeros((7, CHANNELS), taps.dtype)
    offsets = []
    for offset in range(10):
        offsets.append(
            jnp.stack([taps[:, offset - out] if 0 <= offset - out < 7 else empty for out in range(4)], 1)
        )
    table = jnp.stack(offsets, 1)
    return table.reshape(70, 4, 4, 64).transpose(2, 0, 1, 3).reshape(4, 70, 256)


def ocean_kernel(*refs, wide, layer):
    gather, taps, diagonal, gain, up, down, mask, spread, x = refs[:9]
    if wide:
        top, bot, side, above, below, shift = refs[9:15]
        out, blocks, toeplitz, conv_a, conv_b, normed, kept, line, flags = refs[15:]
    else:
        flux, mixing, out, blocks, toeplitz, conv_a, conv_b, normed, kept = refs[9:]
    rows = ROWS + 6 if wide else ROWS
    chunk_rows = rows // 3
    chunks = 3
    lower = lax.broadcasted_iota(jnp.int32, (48, 128), 1) < 64

    def split_row(cells, row):
        moved = jnp.dot(gather[...], cells, preferred_element_type=F32)
        for k in range(5):
            even = moved[96 * k : 96 * k + 48]
            odd = moved[96 * k + 48 : 96 * k + 96]
            for h in range(2):
                e = even[:, 128 * h : 128 * h + 128]
                o = odd[:, 128 * h : 128 * h + 128]
                blocks[2 * h, k, row] = jnp.where(lower, e, pltpu.roll(o, 64, 1)).astype(BF16)
                blocks[2 * h + 1, k, row] = jnp.where(lower, pltpu.roll(e, 64, 1), o).astype(BF16)
        return moved[144:336].astype(BF16)

    def wide_row(cells, halo, row, slot):
        line[slot, 0:180] = cells
        line[slot, 192:208] = halo
        return split_row(line[slot], row)

    def prepare(row):
        if not wide:
            own = split_row(x[row], row)
        elif row < 6:
            own = wide_row(top[row], above[row], row, row % PREP)
        elif row < ROWS + 6:
            own = wide_row(x[row - 6], side[row - 6], row, row % PREP)
        else:
            own = wide_row(bot[row - ROWS - 6], below[row - ROWS - 6], row, row % PREP)
        if 3 <= row < rows + 3:
            kept[row - 3] = own

    if wide:
        for slot in range(PREP):
            line[slot, 176:192] = jnp.zeros((16, CHANNELS), BF16)
        flags[176:192] = jnp.zeros((16, 128), F32)
        flags[0:180] = mask[...] + top[6, :, 0:128].astype(F32) + bot[6, :, 0:128].astype(F32)
        flags[192:208] = (
            side[30, :, 0:128].astype(F32)
            + above[6, :, 0:128].astype(F32)
            + below[6, :, 0:128].astype(F32)
        )
        keep_all = jnp.dot(shift[...], flags[...].astype(BF16), preferred_element_type=F32)
    else:
        keep_all = mask[...]
    for row in range(chunk_rows + 6):
        prepare(row)
    on_diagonal = diagonal[...] != 0

    def build(group, carry):
        toeplitz[group, 35 * 128 : 36 * 128] = jnp.zeros((128, 256), BF16)
        for i in range(70):
            toeplitz[group, i * 64 : i * 64 + 64] = jnp.where(
                on_diagonal,
                jnp.broadcast_to(taps[group, i : i + 1, :], (64, 256)),
                jnp.zeros((), BF16),
            )
        return carry

    lax.fori_loop(0, 4, build, 0)

    def convolve(chunk, conv, group):
        first = chunk * chunk_rows

        def half(n):
            n = min(n, 34)
            return blocks[group, n % 5, pl.ds(first + n // 5, chunk_rows)].reshape(chunk_rows * 48, 128)

        total = None
        for pair in range(18):
            piece = jnp.concatenate([half(2 * pair), half(2 * pair + 1)], axis=1)
            term = jnp.dot(
                piece, toeplitz[group, pair * 256 : pair * 256 + 256], preferred_element_type=F32
            )
            total = term if total is None else total + term
        conv[group] = total

    def normalise(chunk, conv, r):
        sums = [conv[group, r * 48 : r * 48 + 48] for group in range(4)]
        if not wide:
            force = lax.dot_general(
                flux[chunk * chunk_rows + r],
                mixing[...],
                (((0,), (0,)), ((), ())),
                preferred_element_type=F32,
            )
        for hh in range(2):
            parts = [[None, None], [None, None]]
            for h in range(2):
                a = sums[2 * h][:, 128 * hh : 128 * hh + 128]
                b = sums[2 * h + 1][:, 128 * hh : 128 * hh + 128]
                parts[0][h] = jnp.where(lower, a, pltpu.roll(b, 64, 1))
                parts[1][h] = jnp.where(lower, pltpu.roll(a, 64, 1), b)
            for parity in range(2):
                jo = 2 * hh + parity
                v0, v1 = parts[parity]
                mean = jnp.sum(v0 + v1, axis=-1, keepdims=True) * (1.0 / CHANNELS)
                c0 = v0 - mean
                c1 = v1 - mean
                var = jnp.sum(c0 * c0 + c1 * c1, axis=-1, keepdims=True) * (1.0 / CHANNELS)
                rs = lax.rsqrt(var + EPSILON)
                n0 = c0 * rs * gain[:, 0:128]
                n1 = c1 * rs * gain[:, 128:256]
                at = jo * 48
                if not wide:
                    n0 = n0 + force[at : at + 48, :128]
                    n1 = n1 + force[at : at + 48, 128:]
                normed[r * 192 + at : r * 192 + at + 48, 0:128] = n0.astype(BF16)
                normed[r * 192 + at : r * 192 + at + 48, 128:256] = n1.astype(BF16)

    def mix(chunk):
        hidden = jnp.dot(normed[...], up[layer], preferred_element_type=F32).astype(BF16)
        hidden = scaled_gelu(hidden).astype(BF16)
        branch = jnp.dot(hidden, down[layer], preferred_element_type=F32)
        branch = branch * (0.5 / GELU_SCALE)
        for r in range(chunk_rows):
            row = chunk * chunk_rows + r
            value = (branch[r * 192 : r * 192 + 192] + kept[row].astype(F32)).astype(BF16)
            value = jnp.dot(spread[...], value, preferred_element_type=F32)
            keep = keep_all[:, 3 * (not wide) + row : 3 * (not wide) + row + 1]
            out[row] = (value * keep).astype(BF16)

    def prepare_for(chunk, group):
        first = chunk * chunk_rows + 6
        if chunk < chunks:
            for row in range(group * chunk_rows // 4, (group + 1) * chunk_rows // 4):
                prepare(first + row)

    def overlapped(chunk, conv, before, conv_before):
        done = 0
        for group in range(4):
            convolve(chunk, conv, group)
            prepare_for(chunk + 1, group)
            while done * 4 < (group + 1) * chunk_rows and done < chunk_rows:
                normalise(before, conv_before, done)
                done += 1
        mix(before)

    buffers = (conv_a, conv_b)
    for group in range(4):
        convolve(0, conv_a, group)
        prepare_for(1, group)
    for chunk in range(1, chunks):
        overlapped(chunk, buffers[chunk % 2], chunk - 1, buffers[(chunk - 1) % 2])
    for r in range(chunk_rows):
        normalise(chunks - 1, buffers[(chunks - 1) % 2], r)
    mix(chunks - 1)


def ocean_layer(x, layer, taps, gain, up, down, mask, halo=None, flux=None, mixing=None):
    wide = halo is not None
    gather, spread, diagonal, shift = ocean_tables(wide)
    rows = ROWS + 6 if wide else ROWS
    args = [
        jnp.asarray(gather, BF16),
        expand_taps(taps),
        jnp.asarray(diagonal, BF16),
        gain[None] * GELU_SCALE,
        up,
        down,
        mask,
        jnp.asarray(spread, BF16),
        x,
    ]
    scratch = [
        pltpu.VMEM((4, 5, rows + 6, 48, 128), BF16),
        pltpu.VMEM((4, 36 * 128, 256), BF16),
        pltpu.VMEM((4, rows * 16, 256), F32),
        pltpu.VMEM((4, rows * 16, 256), F32),
        pltpu.VMEM((rows * 64, CHANNELS), BF16),
        pltpu.VMEM((rows, 192, CHANNELS), BF16),
    ]
    if wide:
        args += [*halo, jnp.asarray(shift, BF16)]
        scratch += [pltpu.VMEM((PREP, 208, CHANNELS), BF16), pltpu.VMEM((208, 128), F32)]
    else:
        args += [flux, (mixing * GELU_SCALE).astype(BF16)]
    whole = pl.BlockSpec(memory_space=pltpu.VMEM)
    return pl.pallas_call(
        functools.partial(ocean_kernel, wide=wide, layer=layer),
        in_specs=[whole] * len(args),
        out_specs=whole,
        out_shape=jax.ShapeDtypeStruct((rows, 192 if wide else COLS, CHANNELS), BF16),
        scratch_shapes=scratch,
        compiler_params=pltpu.CompilerParams(vmem_limit_bytes=VMEM_BYTES),
        cost_estimate=pl.CostEstimate(
            flops=2 * 14_000_000_000, bytes_accessed=8_000_000, transcendentals=5_529_600
        ),
    )(*args)


def ring(axis, step, wrap):
    size = lax.axis_size(axis)
    pairs = [(i, i + step) for i in range(size)]
    if wrap:
        return [(i, j % size) for i, j in pairs]
    return [(i, j) for i, j in pairs if 0 <= j < size]


def lanes_at(columns, first):
    return jnp.pad(columns, ((0, 0), (first, CHANNELS - first - columns.shape[1])))[None]


def halos(x, flags):
    over = jnp.concatenate([x[ROWS - 6 :], lanes_at(flags[ROWS - 3 :].T, 0)], 0)
    under = jnp.concatenate([x[:6], lanes_at(flags[:3].T, 33)], 0)
    turned = lanes_at(flags.T, 3)
    top = lax.ppermute(over, "row", ring("row", 1, False))
    bot = lax.ppermute(under, "row", ring("row", -1, False))
    east = jnp.concatenate([x[:, COLS - 6 :], turned[:, COLS - 6 :]], 0)
    west = jnp.concatenate([x[:, :6], turned[:, :6]], 0)
    left = lax.ppermute(east, "col", ring("col", 1, True))
    right = lax.ppermute(west, "col", ring("col", -1, True))
    side = jnp.concatenate([left, right, jnp.zeros((ROWS + 1, 4, CHANNELS), BF16)], 1)
    corner = jnp.concatenate([side[ROWS - 6 : ROWS], lanes_at(side[ROWS, :, 30:33], 0)], 0)
    above = lax.ppermute(corner, "row", ring("row", 1, False))
    corner = jnp.concatenate([side[:6], lanes_at(side[ROWS, :, 3:6], 33)], 0)
    below = lax.ppermute(corner, "row", ring("row", -1, False))
    mask = turned[0, :, :128].astype(F32)
    return mask, (top, bot, side, above, below)


AIR = 384
SPAN_LON = 45
SPAN_LAT = 12
WAVES = 192


def spectral_tables():
    lon = np.arange(360)
    wave = np.arange(WAVES)
    angle = 2.0 * np.pi / 360 * (lon[:, None] * (wave[None, :] % MMAX) % 360)
    zonal = np.where(wave[None, :] < MMAX, np.cos(angle), np.sin(angle)) * math.sqrt(2.0 / 360)
    lat = np.arange(192)
    mode = np.arange(LMODES)
    angle = np.pi / 384 * ((2 * lat[:, None] + 1) * mode[None, :] % 768)
    merid = np.cos(angle) * math.sqrt(2.0 / 192)
    zonal = zonal.astype(np.float32).astype(BF16).astype(np.float32)
    merid = merid.astype(np.float32).astype(BF16).astype(np.float32)
    zf = np.zeros((8, 128, 384), np.float32)
    for q in range(8):
        for t2 in range(2):
            zf[q, t2 * 48 : t2 * 48 + 45, t2 * 192 : t2 * 192 + 192] = zonal[q * 45 : q * 45 + 45]
    mf = np.zeros((3, 2, 16, 8, 16, 8, 3), np.float32)
    by_band = merid.reshape(16, 6, 2, 16, 6)
    for c in range(3):
        for t2 in range(2):
            mf[c, t2, :, :6, :, :6, c] = by_band[:, :, t2].transpose(2, 3, 0, 1)
    place = np.zeros((3, 192, 8, 128), np.float32)
    for c in range(3):
        for q in range(8):
            for k in range(24):
                place[c, q * 24 + k, q, c * 24 + k] = 1
    mi = np.zeros((2, 16, 8, 16, 8), np.float32)
    mi[:, :, :6, :, :6] = by_band.transpose(2, 0, 1, 3, 4)
    zi = np.zeros((8, 3, 128, 8, 48), np.float32)
    for q in range(8):
        for c in range(3):
            zi[q, c, c * 24 : c * 24 + 24, :, :45] = (
                zonal[:, q * 24 : q * 24 + 24].reshape(8, 45, 24).transpose(2, 0, 1)
            )
    return (
        zf,
        mf.reshape(3, 2, 128, 384),
        place.reshape(3, 192, 1024),
        mi.reshape(256, 128),
        zi.reshape(8, 3, 128, 384),
    )


def feature_norm(values, gain_row):
    centred = values - jnp.sum(values, axis=-1, keepdims=True) * (1.0 / AIR)
    spread_sq = jnp.sum(centred * centred, axis=-1, keepdims=True) * (1.0 / AIR)
    return centred * lax.rsqrt(spread_sq + EPSILON) * gain_row


def latitude(air, t):
    return jnp.concatenate([air[t].astype(F32), jnp.zeros((3, AIR), F32)], axis=0)


def air_send_kernel(air, gain, emitter, flux_out, send, flat, work):
    for t in range(SPAN_LAT):
        for c in range(3):
            flat[c, pl.ds(t, 45, stride=12)] = air[t, :, 128 * c : 128 * c + 128].astype(F32)
    flux = lax.dot_general(
        emitter[...],
        jnp.concatenate([flat[c, 0:540] for c in range(3)], axis=1).astype(BF16),
        (((1,), (1,)), ((), ())),
        preferred_element_type=F32,
    )
    for block in range(3):
        flux_out[block] = flux[:, block * 180 : block * 180 + 180].astype(BF16)
    zeros = jnp.zeros((32, AIR), F32)
    for t6 in range(6):
        pieces = []
        for t2 in range(2):
            pieces.append(feature_norm(latitude(air, 2 * t6 + t2), gain[...]))
        pair = jnp.concatenate(pieces + [zeros], axis=0)
        for c in range(3):
            work[pl.ds(t6 * 3 + c, 128, stride=24)] = pair[:, c * 128 : c * 128 + 128].T
    for r in range(18, 24):
        work[pl.ds(r, 128, stride=24)] = jnp.zeros((128, 128), F32)

    def pack(step, carry):
        at = pl.multiple_of(step * 8, 8)
        block = work[pl.ds(pl.multiple_of(step * 192, 192), 192)]
        send[pl.ds(at, 8)] = block.reshape(8, 24, 128).astype(BF16)
        return carry

    lax.fori_loop(0, 16, pack, 0)


def forward_kernel(got, zf, mf, place, send):
    total = None
    for q in range(8):
        part = got[:, q].astype(F32).reshape(384, 128).astype(BF16)
        term = jnp.dot(part, zf[q], preferred_element_type=F32)
        total = term if total is None else total + term
    total = total.astype(BF16)
    moved = None
    for c in range(3):
        modes = None
        for t2 in range(2):
            term = jnp.dot(
                mf[c, t2], total[:, t2 * 192 : t2 * 192 + 192], preferred_element_type=F32
            )
            modes = term if modes is None else modes + term
        term = jnp.dot(modes.astype(BF16), place[c], preferred_element_type=F32)
        moved = term if moved is None else moved + term
    for r in range(16):
        for q in range(8):
            send[r * 8 + q] = moved[8 * r : 8 * r + 8, 128 * q : 128 * q + 128].astype(BF16)


def filter_kernel(got, mixing, send, work):
    work[...] = got[...].astype(F32).reshape(1024, 128)
    zeros = jnp.zeros((56, 128), F32)
    results = []
    for mode in range(6):
        turned = work[pl.ds(mode, 128, stride=8)].T
        lhs = jnp.concatenate([turned[24 * c : 24 * c + 24] for c in range(3)], axis=1)
        result = jnp.dot(lhs.astype(BF16), mixing[mode], preferred_element_type=F32)
        stacked = [result[:, 128 * c : 128 * c + 128] for c in range(3)]
        results.append(jnp.concatenate(stacked + [zeros], axis=0).T)
    for mode in range(6):
        work[pl.ds(mode, 128, stride=8)] = results[mode]
    for mode in range(6, 8):
        work[pl.ds(mode, 128, stride=8)] = jnp.zeros((128, 128), F32)
    send[...] = work[...].reshape(128, 8, 128).astype(BF16)


def inverse_kernel(got, mi, zi, send):
    totals = [None, None, None]
    for q in range(8):
        part = got[:, q].astype(F32).reshape(128, 128).astype(BF16)
        bands = jnp.dot(mi[...], part, preferred_element_type=F32).astype(BF16)
        for c in range(3):
            term = jnp.dot(bands, zi[q, c], preferred_element_type=F32)
            totals[c] = term if totals[c] is None else totals[c] + term
    zeros = jnp.zeros((8, 32), F32)
    for c in range(3):
        for r in range(16):
            first = totals[c][8 * r : 8 * r + 8]
            second = totals[c][128 + 8 * r : 128 + 8 * r + 8]
            for q in range(8):
                row = jnp.concatenate(
                    [first[:, 48 * q : 48 * q + 48], second[:, 48 * q : 48 * q + 48], zeros], axis=1
                )
                send[r * 8 + q, 8 * c : 8 * c + 8] = row.astype(BF16)


def air_finish_kernel(got, air, gain, sst, heat, up, down, out, work, mid):
    work[...] = got[...].astype(F32).reshape(128 * 24, 128)
    entries = []
    for t6 in range(6):
        turned = [work[pl.ds(8 * c + t6, 128, stride=24)].T for c in range(3)]
        for t2 in range(2):
            t = 2 * t6 + t2
            spectral = jnp.concatenate([v[48 * t2 : 48 * t2 + 48] for v in turned], axis=1)
            value = latitude(air, t) + spectral
            mid[48 * t : 48 * t + 48] = value
            entry = feature_norm(value, gain[...]) + sst[:, t : t + 1] * heat[...]
            entries.append(entry.astype(BF16))
    entry = jnp.concatenate(entries, axis=0)
    hidden = jnp.dot(entry, up[...], preferred_element_type=F32)
    hidden = jax.nn.gelu(hidden, approximate=True).astype(BF16)
    result = mid[...] + jnp.dot(hidden, down[...], preferred_element_type=F32)
    for t in range(SPAN_LAT):
        out[t] = result[48 * t : 48 * t + 45].astype(BF16)


def plain_kernel(kernel, outs, scratch, flops, *args):
    whole = pl.BlockSpec(memory_space=pltpu.VMEM)
    size = sum(math.prod(a.shape) * a.dtype.itemsize for a in args)
    return pl.pallas_call(
        kernel,
        in_specs=[whole] * len(args),
        out_specs=[whole] * len(outs),
        out_shape=[jax.ShapeDtypeStruct(s, BF16) for s in outs],
        scratch_shapes=[pltpu.VMEM(s, F32) for s in scratch],
        compiler_params=pltpu.CompilerParams(vmem_limit_bytes=VMEM_BYTES),
        cost_estimate=pl.CostEstimate(flops=flops, bytes_accessed=size, transcendentals=0),
    )(*args)


def swap(message):
    return lax.all_to_all(message, ("row", "col"), 0, 0, tiled=True)


def spectral_chain(message, harmonic):
    zf, mf, place, mi, zi = [jnp.asarray(t, BF16) for t in spectral_tables()]
    got = swap(message).reshape(16, 8, 24, 128)
    (message,) = plain_kernel(
        forward_kernel, [(128, 8, 128)], [], 2_000_000_000, got, zf, mf, place
    )
    got = swap(message)
    (message,) = plain_kernel(
        filter_kernel, [(128, 8, 128)], [(1024, 128)], 500_000_000, got, harmonic
    )
    got = swap(message).reshape(16, 8, 8, 128)
    (message,) = plain_kernel(inverse_kernel, [(128, 24, 128)], [], 2_000_000_000, got, mi, zi)
    return swap(message)


def body(
    sea_fields_now,
    water_site_flags,
    separable_stencils,
    sea_scaling_factors,
    sea_first_matrices,
    sea_second_matrices,
    exchange_to_sea_matrix,
    heat_emitter,
    air_fields_now,
    air_scaling_factors,
    harmonic_combine_matrix,
    air_first_matrix,
    air_second_matrix,
    exchange_emitter,
    heat_to_air_matrix,
    regrid_area_factors,
    link_regrid_group,
    patch_active_links,
):
    row_pos = lax.axis_index("row")
    col_pos = lax.axis_index("col")
    row_total = lax.axis_size("row")
    strip_meridian_number, strip_parallel_number, atmos_width = air_fields_now.shape
    tile_rows, tile_cols, ocean_channel_count = sea_fields_now.shape
    block_cells = strip_meridian_number // REGRID_GROUPS * strip_parallel_number
    block_total = row_total * REGRID_GROUPS
    air_bands = air_fields_now.transpose(1, 0, 2)
    flux_blocks, message = plain_kernel(
        air_send_kernel,
        [(3, NF, 180), (128, 24, 128)],
        [(3, 576, 128), (3072, 128)],
        100_000_000,
        air_bands,
        air_scaling_factors[0:1],
        exchange_emitter.T,
    )
    heat_site_values = jnp.einsum(
        "yxc,c->yx", sea_fields_now, heat_emitter, preferred_element_type=F32
    )
    heat_site_values = (heat_site_values * water_site_flags.astype(F32)).astype(BF16).reshape(-1)
    column_pairs = link_regrid_group[:, 0, :]
    column_counts = patch_active_links[:, 0]
    own_pairs = lax.dynamic_index_in_dim(column_pairs, row_pos, 0, keepdims=False)
    own_count = lax.dynamic_index_in_dim(column_counts, row_pos, 0, keepdims=False)
    pair_slots = jnp.arange(PATCH_LINK_ROOM, dtype=jnp.int32)
    link_active_flag = pair_slots < own_count
    own_link_factors = regrid_area_factors[0, 0]
    link_heat_values = jnp.einsum(
        "hnc,c->hn", own_link_factors, heat_site_values, preferred_element_type=jnp.float32
    )
    link_heat_values = (link_heat_values * link_active_flag[:, None].astype(jnp.float32)).astype(
        jnp.bfloat16
    )
    parcel = jnp.concatenate(
        [flux_blocks, link_heat_values[:, None, :], jnp.zeros((3, 39, block_cells), BF16)], 1
    )
    parcel = jnp.pad(parcel, ((0, 0), (0, 0), (0, 256 - block_cells)))
    gathered = lax.all_gather(parcel, "row", axis=0, tiled=True)
    pick_pairs = (
        link_active_flag[:, None]
        & (own_pairs[:, None] == jnp.arange(block_total, dtype=jnp.int32)[None, :])
    ).astype(BF16)
    chosen = jnp.einsum(
        "pq,qfa->pfa", pick_pairs, gathered[:, :NF, :block_cells], preferred_element_type=F32
    )
    own_blocks = row_pos * REGRID_GROUPS + jnp.arange(REGRID_GROUPS, dtype=jnp.int32)
    landing = (own_blocks[:, None] == column_pairs.reshape(1, -1)).astype(BF16)
    own_heat_values = jnp.dot(
        landing, gathered[:, NF, :block_cells], preferred_element_type=F32
    )
    sea_exchange_values = jnp.einsum(
        "pfa,pao->fo",
        chosen.astype(BF16),
        own_link_factors,
        preferred_element_type=F32,
    )
    flux_rows = sea_exchange_values.astype(BF16).reshape(NF, ROWS, COLS)
    flux_rows = jnp.pad(flux_rows, ((0, 0), (0, 0), (0, 12))).reshape(NF, ROWS, 48, 4)
    flux_rows = flux_rows.transpose(1, 0, 3, 2).reshape(ROWS, NF, 192)
    heat_lattice = jnp.pad(
        own_heat_values.reshape(strip_meridian_number, strip_parallel_number), ((0, 3), (0, 0))
    )
    spectral = spectral_chain(message, harmonic_combine_matrix)
    (air_fields_next,) = plain_kernel(
        air_finish_kernel,
        [air_bands.shape],
        [(3072, 128), (576, AIR)],
        700_000_000,
        spectral,
        air_bands,
        air_scaling_factors[1:2],
        heat_lattice,
        heat_to_air_matrix[None],
        air_first_matrix,
        air_second_matrix,
    )
    mask, halo = halos(sea_fields_now, water_site_flags.astype(BF16))
    layers = []
    for layer in range(LAYERS):
        layers.append(
            (
                layer,
                separable_stencils[layer],
                sea_scaling_factors[layer],
                sea_first_matrices,
                sea_second_matrices,
                mask,
            )
        )
    current = ocean_layer(sea_fields_now, *layers[0], halo=halo)
    current = ocean_layer(current, *layers[1], flux=flux_rows, mixing=exchange_to_sea_matrix)
    return (current, air_fields_next.transpose(1, 0, 2))


def solution(mesh):
    in_specs = (
        P("row", "col", None),
        P("row", "col"),
        P(),
        P(),
        P(),
        P(),
        P(),
        P(),
        P("col", "row", None),
        P(),
        P("row", None, None),
        P(),
        P(),
        P(),
        P(),
        P("row", "col", None, None, None),
        P(None, "col", None),
        P(None, "col"),
    )
    out_specs = (P("row", "col", None), P("col", "row", None))
    return jax.shard_map(body, mesh=mesh, in_specs=in_specs, out_specs=out_specs, check_vma=False)
```

```python
import functools
import math

import jax
import jax.numpy as jnp
import numpy as np
from jax import lax
from jax.experimental import pallas as pl
from jax.experimental.pallas import tpu as pltpu
from jax.sharding import PartitionSpec as P

NF = 8
MERIDIAN_TOTAL = 360
MMAX = 96
LMODES = 96
LAYERS = 2
REGRID_GROUPS = 3
PATCH_LINK_ROOM = 3


EPSILON = 1e-06
HIGHEST_MODE = lax.Precision.HIGHEST


BF16 = jnp.bfloat16
F32 = jnp.float32
GELU_SLOPE = math.sqrt(2.0 / math.pi)
GELU_SCALE = (GELU_SLOPE * 0.044715) ** (1.0 / 3.0)
GELU_LINEAR = GELU_SLOPE / GELU_SCALE
VMEM_BYTES = 60 * 1024 * 1024
ROWS = 30
COLS = 180
CHANNELS = 256
PREP = 6
CHUNKS = 3


def scaled_gelu(scaled):
    inner = (scaled * scaled + GELU_LINEAR) * scaled
    return scaled + scaled * jnp.tanh(inner)


def ocean_tables(wide):
    reach = 6 if wide else 0
    width = 208 if wide else 192
    gather = np.zeros((480, width), np.float32)
    for shift in range(10):
        for block in range(48):
            place = 4 * block + shift - reach
            if wide and -6 <= place < 0:
                place = 192 + place + 6
            elif wide and COLS <= place < COLS + 6:
                place = 198 + place - COLS
            elif not 0 <= place < (COLS if wide else COLS + 6):
                continue
            gather[shift * 48 + block, place] = 1
    cells = 192 if wide else COLS
    spread = np.zeros((cells, 192), np.float32)
    for place in range(cells):
        spread[place, (place % 4) * 48 + place // 4] = 1
    shift = np.zeros((192, 208), np.float32)
    for cell in range(-3, COLS + 3):
        source = 192 + cell + 6 if cell < 0 else 198 + cell - COLS if cell >= COLS else cell
        shift[cell + 3, source] = 1
    diagonal = np.tile(np.eye(64, dtype=np.float32), (1, 4))
    return gather, spread, diagonal, shift


def expand_taps(taps):
    padded = jnp.pad(taps, ((0, 0), (0, 0), (3, 3), (0, 0)))
    table = jnp.stack([padded[:, :, 3 - out : 13 - out] for out in range(4)], 3)
    table = table.reshape(LAYERS, 70, 4, 4, 64).transpose(0, 3, 1, 2, 4)
    return table.reshape(LAYERS, 4, 70, 256)


def ocean_kernel(*refs, wide, layer):
    gather, taps, diagonal, gain, up, down, mask, spread, x = refs[:9]
    if wide:
        top, bot, side, shift = refs[9:13]
        out, blocks, toeplitz, conv_a, conv_b, normed, kept, line, flags = refs[13:]
    else:
        flux, mixing, out, blocks, toeplitz, conv_a, conv_b, normed, kept = refs[9:]
    rows = ROWS + 6 if wide else ROWS
    chunk_rows = rows // CHUNKS
    chunks = CHUNKS
    lower = lax.broadcasted_iota(jnp.int32, (48, 128), 1) < 64

    def split_row(cells, row):
        moved = jnp.dot(gather[...], cells, preferred_element_type=F32)
        for k in range(5):
            even = moved[96 * k : 96 * k + 48]
            odd = moved[96 * k + 48 : 96 * k + 96]
            for h in range(2):
                e = even[:, 128 * h : 128 * h + 128]
                o = odd[:, 128 * h : 128 * h + 128]
                blocks[2 * h, k, row] = jnp.where(lower, e, pltpu.roll(o, 64, 1)).astype(BF16)
                blocks[2 * h + 1, k, row] = jnp.where(lower, pltpu.roll(e, 64, 1), o).astype(BF16)
        return moved[144:336].astype(BF16)

    def wide_row(cells, halo, row, slot):
        line[slot, 0:180] = cells
        line[slot, 192:208] = halo
        return split_row(line[slot], row)

    def prepare(row):
        if not wide:
            own = split_row(x[row], row)
        elif row < 6:
            own = wide_row(top[row, 16:196], top[row, 0:16], row, row % PREP)
        elif row < ROWS + 6:
            own = wide_row(x[row - 6], side[row - 6], row, row % PREP)
        else:
            at = row - ROWS - 6
            own = wide_row(bot[at, 16:196], bot[at, 0:16], row, row % PREP)
        if 3 <= row < rows + 3:
            kept[row - 3] = own

    if wide:
        for slot in range(PREP):
            line[slot, 176:192] = jnp.zeros((16, CHANNELS), BF16)
        flags[176:192] = jnp.zeros((16, 128), F32)
        edges = top[6, :, 0:128].astype(F32) + bot[6, :, 0:128].astype(F32)
        flags[0:180] = mask[...] + edges[16:196]
        flags[192:208] = side[30, :, 0:128].astype(F32) + edges[0:16]
        keep_all = jnp.dot(shift[...], flags[...].astype(BF16), preferred_element_type=F32)
    else:
        keep_all = mask[...]
    for row in range(chunk_rows + 6):
        prepare(row)
    on_diagonal = diagonal[...] != 0

    def build(group, carry):
        toeplitz[group, 35 * 128 : 36 * 128] = jnp.zeros((128, 256), BF16)
        for i in range(70):
            toeplitz[group, i * 64 : i * 64 + 64] = jnp.where(
                on_diagonal,
                jnp.broadcast_to(taps[layer, group, i : i + 1, :], (64, 256)),
                jnp.zeros((), BF16),
            )
        return carry

    lax.fori_loop(0, 4, build, 0)

    def convolve(chunk, conv, group):
        first = chunk * chunk_rows

        def half(n):
            n = min(n, 34)
            return blocks[group, n % 5, pl.ds(first + n // 5, chunk_rows)].reshape(chunk_rows * 48, 128)

        total = None
        for pair in range(18):
            piece = jnp.concatenate([half(2 * pair), half(2 * pair + 1)], axis=1)
            term = jnp.dot(
                piece, toeplitz[group, pair * 256 : pair * 256 + 256], preferred_element_type=F32
            )
            total = term if total is None else total + term
        conv[group] = total

    def normalise(chunk, conv, r):
        sums = [conv[group, r * 48 : r * 48 + 48] for group in range(4)]
        if not wide:
            force = lax.dot_general(
                flux[chunk * chunk_rows + r],
                mixing[...],
                (((0,), (0,)), ((), ())),
                preferred_element_type=F32,
            )
        for hh in range(2):
            parts = [[None, None], [None, None]]
            for h in range(2):
                a = sums[2 * h][:, 128 * hh : 128 * hh + 128]
                b = sums[2 * h + 1][:, 128 * hh : 128 * hh + 128]
                parts[0][h] = jnp.where(lower, a, pltpu.roll(b, 64, 1))
                parts[1][h] = jnp.where(lower, pltpu.roll(a, 64, 1), b)
            for parity in range(2):
                jo = 2 * hh + parity
                v0, v1 = parts[parity]
                mean = jnp.sum(v0 + v1, axis=-1, keepdims=True) * (1.0 / CHANNELS)
                c0 = v0 - mean
                c1 = v1 - mean
                var = jnp.sum(c0 * c0 + c1 * c1, axis=-1, keepdims=True) * (1.0 / CHANNELS)
                rs = lax.rsqrt(var + EPSILON)
                n0 = c0 * rs * gain[:, 0:128]
                n1 = c1 * rs * gain[:, 128:256]
                at = jo * 48
                if not wide:
                    n0 = n0 + force[at : at + 48, :128]
                    n1 = n1 + force[at : at + 48, 128:]
                normed[r * 192 + at : r * 192 + at + 48, 0:128] = n0.astype(BF16)
                normed[r * 192 + at : r * 192 + at + 48, 128:256] = n1.astype(BF16)

    def mix(chunk):
        hidden = jnp.dot(normed[...], up[layer], preferred_element_type=F32).astype(BF16)
        hidden = scaled_gelu(hidden).astype(BF16)
        branch = jnp.dot(hidden, down[layer], preferred_element_type=F32)
        branch = branch * (0.5 / GELU_SCALE)
        for r in range(chunk_rows):
            row = chunk * chunk_rows + r
            value = (branch[r * 192 : r * 192 + 192] + kept[row].astype(F32)).astype(BF16)
            value = jnp.dot(spread[...], value, preferred_element_type=F32)
            keep = keep_all[:, 3 * (not wide) + row : 3 * (not wide) + row + 1]
            out[row] = (value * keep).astype(BF16)

    def prepare_for(chunk, group):
        first = chunk * chunk_rows + 6
        if chunk < chunks:
            for row in range(group * chunk_rows // 4, (group + 1) * chunk_rows // 4):
                prepare(first + row)

    def overlapped(chunk, conv, before, conv_before):
        done = 0
        for group in range(4):
            convolve(chunk, conv, group)
            prepare_for(chunk + 1, group)
            while done * 4 < (group + 1) * chunk_rows and done < chunk_rows:
                normalise(before, conv_before, done)
                done += 1
        mix(before)

    buffers = (conv_a, conv_b)
    for group in range(4):
        convolve(0, conv_a, group)
        prepare_for(1, group)
    for chunk in range(1, chunks):
        overlapped(chunk, buffers[chunk % 2], chunk - 1, buffers[(chunk - 1) % 2])
    for r in range(chunk_rows):
        normalise(chunks - 1, buffers[(chunks - 1) % 2], r)
    mix(chunks - 1)


def ocean_layer(x, layer, taps, gain, up, down, mask, halo=None, flux=None, mixing=None):
    wide = halo is not None
    gather, spread, diagonal, shift = ocean_tables(wide)
    rows = ROWS + 6 if wide else ROWS
    args = [
        jnp.asarray(gather, BF16),
        taps,
        jnp.asarray(diagonal, BF16),
        gain[None] * GELU_SCALE,
        up,
        down,
        mask,
        jnp.asarray(spread, BF16),
        x,
    ]
    scratch = [
        pltpu.VMEM((4, 5, rows + 6, 48, 128), BF16),
        pltpu.VMEM((4, 36 * 128, 256), BF16),
        pltpu.VMEM((4, rows // CHUNKS * 48, 256), F32),
        pltpu.VMEM((4, rows // CHUNKS * 48, 256), F32),
        pltpu.VMEM((rows // CHUNKS * 192, CHANNELS), BF16),
        pltpu.VMEM((rows, 192, CHANNELS), BF16),
    ]
    if wide:
        args += [*halo, jnp.asarray(shift, BF16)]
        scratch += [pltpu.VMEM((PREP, 208, CHANNELS), BF16), pltpu.VMEM((208, 128), F32)]
    else:
        args += [flux, (mixing * GELU_SCALE).astype(BF16)]
    whole = pl.BlockSpec(memory_space=pltpu.VMEM)
    return pl.pallas_call(
        functools.partial(ocean_kernel, wide=wide, layer=layer),
        in_specs=[whole] * len(args),
        out_specs=whole,
        out_shape=jax.ShapeDtypeStruct((rows, 192 if wide else COLS, CHANNELS), BF16),
        scratch_shapes=scratch,
        compiler_params=pltpu.CompilerParams(vmem_limit_bytes=VMEM_BYTES),
        cost_estimate=pl.CostEstimate(
            flops=2 * 14_000_000_000, bytes_accessed=8_000_000, transcendentals=5_529_600
        ),
    )(*args)


def ring(axis, step, wrap):
    size = lax.axis_size(axis)
    pairs = [(i, i + step) for i in range(size)]
    if wrap:
        return [(i, j % size) for i, j in pairs]
    return [(i, j) for i, j in pairs if 0 <= j < size]


def lanes_at(columns, first):
    return jnp.pad(columns, ((0, 0), (first, CHANNELS - first - columns.shape[1])))[None]


def halos(x, flags):
    turned = lanes_at(flags.T, 3)
    east = jnp.concatenate([x[:, COLS - 6 :], turned[:, COLS - 6 :]], 0)
    west = jnp.concatenate([x[:, :6], turned[:, :6]], 0)
    left = lax.ppermute(east, "col", ring("col", 1, True))
    right = lax.ppermute(west, "col", ring("col", -1, True))
    side = jnp.concatenate([left, right, jnp.zeros((ROWS + 1, 4, CHANNELS), BF16)], 1)

    def message(first, flag_rows, lane):
        cells = jnp.concatenate([side[first : first + 6], x[first : first + 6]], 1)
        near = side[ROWS, :, 3 + flag_rows : 6 + flag_rows]
        own = flags[flag_rows : flag_rows + 3].T
        return jnp.concatenate([cells, lanes_at(jnp.concatenate([near, own], 0), lane)], 0)

    top = lax.ppermute(message(ROWS - 6, ROWS - 3, 0), "row", ring("row", 1, False))
    bot = lax.ppermute(message(0, 0, 33), "row", ring("row", -1, False))
    mask = turned[0, :, :128].astype(F32)
    return mask, (top, bot, side)


AIR = 384
SPAN_LON = 45
SPAN_LAT = 12
WAVES = 192


def spectral_tables():
    lon = np.arange(360)
    wave = np.arange(WAVES)
    angle = 2.0 * np.pi / 360 * (lon[:, None] * (wave[None, :] % MMAX) % 360)
    zonal = np.where(wave[None, :] < MMAX, np.cos(angle), np.sin(angle)) * math.sqrt(2.0 / 360)
    lat = np.arange(192)
    mode = np.arange(LMODES)
    angle = np.pi / 384 * ((2 * lat[:, None] + 1) * mode[None, :] % 768)
    merid = np.cos(angle) * math.sqrt(2.0 / 192)
    zonal = zonal.astype(np.float32).astype(BF16).astype(np.float32)
    merid = merid.astype(np.float32).astype(BF16).astype(np.float32)
    zf = np.zeros((8, 128, 384), np.float32)
    for q in range(8):
        for t2 in range(2):
            zf[q, t2 * 48 : t2 * 48 + 45, t2 * 192 : t2 * 192 + 192] = zonal[q * 45 : q * 45 + 45]
    mf = np.zeros((3, 2, 16, 8, 16, 8, 3), np.float32)
    by_band = merid.reshape(16, 6, 2, 16, 6)
    for c in range(3):
        for t2 in range(2):
            mf[c, t2, :, :6, :, :6, c] = by_band[:, :, t2].transpose(2, 3, 0, 1)
    place = np.zeros((3, 192, 8, 128), np.float32)
    for c in range(3):
        for q in range(8):
            for k in range(24):
                place[c, q * 24 + k, q, c * 24 + k] = 1
    mi = np.zeros((2, 16, 8, 16, 8), np.float32)
    mi[:, :, :6, :, :6] = by_band.transpose(2, 0, 1, 3, 4)
    zi = np.zeros((8, 3, 128, 8, 48), np.float32)
    for q in range(8):
        for c in range(3):
            zi[q, c, c * 24 : c * 24 + 24, :, :45] = (
                zonal[:, q * 24 : q * 24 + 24].reshape(8, 45, 24).transpose(2, 0, 1)
            )
    return (
        zf,
        mf.reshape(3, 2, 128, 384),
        place.reshape(3, 192, 1024),
        mi.reshape(256, 128),
        zi.reshape(8, 3, 128, 384),
    )


def feature_norm(values, gain_row):
    centred = values - jnp.sum(values, axis=-1, keepdims=True) * (1.0 / AIR)
    spread_sq = jnp.sum(centred * centred, axis=-1, keepdims=True) * (1.0 / AIR)
    return centred * lax.rsqrt(spread_sq + EPSILON) * gain_row


def latitude(air, t):
    return jnp.concatenate([air[t].astype(F32), jnp.zeros((3, AIR), F32)], axis=0)


def air_send_kernel(air, gain, emitter, flux_out, send, flat, work):
    for t in range(SPAN_LAT):
        for c in range(3):
            flat[c, pl.ds(t, 45, stride=12)] = air[t, :, 128 * c : 128 * c + 128].astype(F32)
    flux = lax.dot_general(
        emitter[...],
        jnp.concatenate([flat[c, 0:540] for c in range(3)], axis=1).astype(BF16),
        (((1,), (1,)), ((), ())),
        preferred_element_type=F32,
    )
    for block in range(3):
        flux_out[block] = flux[:, block * 180 : block * 180 + 180].astype(BF16)
    zeros = jnp.zeros((32, AIR), F32)
    for t6 in range(6):
        pieces = []
        for t2 in range(2):
            pieces.append(feature_norm(latitude(air, 2 * t6 + t2), gain[...]))
        pair = jnp.concatenate(pieces + [zeros], axis=0)
        for c in range(3):
            work[pl.ds(t6 * 3 + c, 128, stride=24)] = pair[:, c * 128 : c * 128 + 128].T
    for r in range(18, 24):
        work[pl.ds(r, 128, stride=24)] = jnp.zeros((128, 128), F32)

    def pack(step, carry):
        at = pl.multiple_of(step * 8, 8)
        block = work[pl.ds(pl.multiple_of(step * 192, 192), 192)]
        send[pl.ds(at, 8)] = block.reshape(8, 24, 128).astype(BF16)
        return carry

    lax.fori_loop(0, 16, pack, 0)


def forward_kernel(got, zf, mf, place, send):
    total = None
    for q in range(8):
        part = got[:, q].astype(F32).reshape(384, 128).astype(BF16)
        term = jnp.dot(part, zf[q], preferred_element_type=F32)
        total = term if total is None else total + term
    total = total.astype(BF16)
    moved = None
    for c in range(3):
        modes = None
        for t2 in range(2):
            term = jnp.dot(
                mf[c, t2], total[:, t2 * 192 : t2 * 192 + 192], preferred_element_type=F32
            )
            modes = term if modes is None else modes + term
        term = jnp.dot(modes.astype(BF16), place[c], preferred_element_type=F32)
        moved = term if moved is None else moved + term
    for r in range(16):
        for q in range(8):
            send[r * 8 + q] = moved[8 * r : 8 * r + 8, 128 * q : 128 * q + 128].astype(BF16)


def filter_kernel(got, mixing, send, work):
    work[...] = got[...].astype(F32).reshape(1024, 128)
    zeros = jnp.zeros((56, 128), F32)
    results = []
    for mode in range(6):
        turned = work[pl.ds(mode, 128, stride=8)].T
        lhs = jnp.concatenate([turned[24 * c : 24 * c + 24] for c in range(3)], axis=1)
        result = jnp.dot(lhs.astype(BF16), mixing[mode], preferred_element_type=F32)
        stacked = [result[:, 128 * c : 128 * c + 128] for c in range(3)]
        results.append(jnp.concatenate(stacked + [zeros], axis=0).T)
    for mode in range(6):
        work[pl.ds(mode, 128, stride=8)] = results[mode]
    for mode in range(6, 8):
        work[pl.ds(mode, 128, stride=8)] = jnp.zeros((128, 128), F32)
    send[...] = work[...].reshape(128, 8, 128).astype(BF16)


def inverse_kernel(got, mi, zi, send):
    totals = [None, None, None]
    for q in range(8):
        part = got[:, q].astype(F32).reshape(128, 128).astype(BF16)
        bands = jnp.dot(mi[...], part, preferred_element_type=F32).astype(BF16)
        for c in range(3):
            term = jnp.dot(bands, zi[q, c], preferred_element_type=F32)
            totals[c] = term if totals[c] is None else totals[c] + term
    zeros = jnp.zeros((8, 32), F32)
    for c in range(3):
        for r in range(16):
            first = totals[c][8 * r : 8 * r + 8]
            second = totals[c][128 + 8 * r : 128 + 8 * r + 8]
            for q in range(8):
                row = jnp.concatenate(
                    [first[:, 48 * q : 48 * q + 48], second[:, 48 * q : 48 * q + 48], zeros], axis=1
                )
                send[r * 8 + q, 8 * c : 8 * c + 8] = row.astype(BF16)


def air_finish_kernel(got, air, gain, sst, heat, up, down, out, work, mid):
    work[...] = got[...].astype(F32).reshape(128 * 24, 128)
    entries = []
    for t6 in range(6):
        turned = [work[pl.ds(8 * c + t6, 128, stride=24)].T for c in range(3)]
        for t2 in range(2):
            t = 2 * t6 + t2
            spectral = jnp.concatenate([v[48 * t2 : 48 * t2 + 48] for v in turned], axis=1)
            value = latitude(air, t) + spectral
            mid[48 * t : 48 * t + 48] = value
            entry = feature_norm(value, gain[...]) + sst[:, t : t + 1] * heat[...]
            entries.append(entry.astype(BF16))
    entry = jnp.concatenate(entries, axis=0)
    hidden = jnp.dot(entry, up[...], preferred_element_type=F32)
    hidden = jax.nn.gelu(hidden, approximate=True).astype(BF16)
    result = mid[...] + jnp.dot(hidden, down[...], preferred_element_type=F32)
    for t in range(SPAN_LAT):
        out[t] = result[48 * t : 48 * t + 45].astype(BF16)


def plain_kernel(kernel, outs, scratch, flops, *args):
    whole = pl.BlockSpec(memory_space=pltpu.VMEM)
    size = sum(math.prod(a.shape) * a.dtype.itemsize for a in args)
    return pl.pallas_call(
        kernel,
        in_specs=[whole] * len(args),
        out_specs=[whole] * len(outs),
        out_shape=[jax.ShapeDtypeStruct(s, BF16) for s in outs],
        scratch_shapes=[pltpu.VMEM(s, F32) for s in scratch],
        compiler_params=pltpu.CompilerParams(vmem_limit_bytes=VMEM_BYTES),
        cost_estimate=pl.CostEstimate(flops=flops, bytes_accessed=size, transcendentals=0),
    )(*args)


def swap(message):
    return lax.all_to_all(message, ("row", "col"), 0, 0, tiled=True)


def spectral_chain(message, harmonic):
    zf, mf, place, mi, zi = [jnp.asarray(t, BF16) for t in spectral_tables()]
    got = swap(message).reshape(16, 8, 24, 128)
    (message,) = plain_kernel(
        forward_kernel, [(128, 8, 128)], [], 2_000_000_000, got, zf, mf, place
    )
    got = swap(message)
    (message,) = plain_kernel(
        filter_kernel, [(128, 8, 128)], [(1024, 128)], 500_000_000, got, harmonic
    )
    got = swap(message).reshape(16, 8, 8, 128)
    (message,) = plain_kernel(inverse_kernel, [(128, 24, 128)], [], 2_000_000_000, got, mi, zi)
    return swap(message)


def body(
    sea_fields_now,
    water_site_flags,
    separable_stencils,
    sea_scaling_factors,
    sea_first_matrices,
    sea_second_matrices,
    exchange_to_sea_matrix,
    heat_emitter,
    air_fields_now,
    air_scaling_factors,
    harmonic_combine_matrix,
    air_first_matrix,
    air_second_matrix,
    exchange_emitter,
    heat_to_air_matrix,
    regrid_area_factors,
    link_regrid_group,
    patch_active_links,
):
    row_pos = lax.axis_index("row")
    col_pos = lax.axis_index("col")
    row_total = lax.axis_size("row")
    strip_meridian_number, strip_parallel_number, atmos_width = air_fields_now.shape
    tile_rows, tile_cols, ocean_channel_count = sea_fields_now.shape
    block_cells = strip_meridian_number // REGRID_GROUPS * strip_parallel_number
    block_total = row_total * REGRID_GROUPS
    air_bands = air_fields_now.transpose(1, 0, 2)
    flux_blocks, message = plain_kernel(
        air_send_kernel,
        [(3, NF, 180), (128, 24, 128)],
        [(3, 576, 128), (3072, 128)],
        100_000_000,
        air_bands,
        air_scaling_factors[0:1],
        exchange_emitter.T,
    )
    heat_site_values = jnp.einsum(
        "yxc,c->yx", sea_fields_now, heat_emitter, preferred_element_type=F32
    )
    heat_site_values = (heat_site_values * water_site_flags.astype(F32)).astype(BF16).reshape(-1)
    column_pairs = link_regrid_group[:, 0, :]
    column_counts = patch_active_links[:, 0]
    own_pairs = lax.dynamic_index_in_dim(column_pairs, row_pos, 0, keepdims=False)
    own_count = lax.dynamic_index_in_dim(column_counts, row_pos, 0, keepdims=False)
    pair_slots = jnp.arange(PATCH_LINK_ROOM, dtype=jnp.int32)
    link_active_flag = pair_slots < own_count
    own_link_factors = regrid_area_factors[0, 0]
    link_heat_values = jnp.einsum(
        "hnc,c->hn", own_link_factors, heat_site_values, preferred_element_type=jnp.float32
    )
    link_heat_values = (link_heat_values * link_active_flag[:, None].astype(jnp.float32)).astype(
        jnp.bfloat16
    )
    parcel = jnp.concatenate(
        [flux_blocks, link_heat_values[:, None, :], jnp.zeros((3, 39, block_cells), BF16)], 1
    )
    parcel = jnp.pad(parcel, ((0, 0), (0, 0), (0, 256 - block_cells)))
    gathered = lax.all_gather(parcel, "row", axis=0, tiled=True)
    pick_pairs = (
        link_active_flag[:, None]
        & (own_pairs[:, None] == jnp.arange(block_total, dtype=jnp.int32)[None, :])
    ).astype(BF16)
    chosen = jnp.einsum(
        "pq,qfa->pfa", pick_pairs, gathered[:, :NF, :block_cells], preferred_element_type=F32
    )
    own_blocks = row_pos * REGRID_GROUPS + jnp.arange(REGRID_GROUPS, dtype=jnp.int32)
    landing = (own_blocks[:, None] == column_pairs.reshape(1, -1)).astype(BF16)
    own_heat_values = jnp.dot(
        landing, gathered[:, NF, :block_cells], preferred_element_type=F32
    )
    sea_exchange_values = jnp.einsum(
        "pfa,pao->fo",
        chosen.astype(BF16),
        own_link_factors,
        preferred_element_type=F32,
    )
    flux_rows = sea_exchange_values.astype(BF16).reshape(NF, ROWS, COLS)
    flux_rows = jnp.pad(flux_rows, ((0, 0), (0, 0), (0, 12))).reshape(NF, ROWS, 48, 4)
    flux_rows = flux_rows.transpose(1, 0, 3, 2).reshape(ROWS, NF, 192)
    heat_lattice = jnp.pad(
        own_heat_values.reshape(strip_meridian_number, strip_parallel_number), ((0, 3), (0, 0))
    )
    spectral = spectral_chain(message, harmonic_combine_matrix)
    (air_fields_next,) = plain_kernel(
        air_finish_kernel,
        [air_bands.shape],
        [(3072, 128), (576, AIR)],
        700_000_000,
        spectral,
        air_bands,
        air_scaling_factors[1:2],
        heat_lattice,
        heat_to_air_matrix[None],
        air_first_matrix,
        air_second_matrix,
    )
    mask, halo = halos(sea_fields_now, water_site_flags.astype(BF16))
    taps = expand_taps(separable_stencils)
    layers = []
    for layer in range(LAYERS):
        layers.append(
            (
                layer,
                taps,
                sea_scaling_factors[layer],
                sea_first_matrices,
                sea_second_matrices,
                mask,
            )
        )
    current = ocean_layer(sea_fields_now, *layers[0], halo=halo)
    current = ocean_layer(current, *layers[1], flux=flux_rows, mixing=exchange_to_sea_matrix)
    return (current, air_fields_next.transpose(1, 0, 2))


def solution(mesh):
    in_specs = (
        P("row", "col", None),
        P("row", "col"),
        P(),
        P(),
        P(),
        P(),
        P(),
        P(),
        P("col", "row", None),
        P(),
        P("row", None, None),
        P(),
        P(),
        P(),
        P(),
        P("row", "col", None, None, None),
        P(None, "col", None),
        P(None, "col"),
    )
    out_specs = (P("row", "col", None), P("col", "row", None))
    return jax.shard_map(body, mesh=mesh, in_specs=in_specs, out_specs=out_specs, check_vma=False)
```
